32 devices in a mesh: rows: 16 (over z, x, core), cols: 2 (over y).
Axes of the slice: x: 2, y: 2, z: 4, core: 2. Of those that a mesh axis runs over, the one named last changes fastest.
Arguments:
- rhs: float32 [3, 32, 256, 128], P(None, 'rows', 'cols'), may hold values from -6 to 6
- diag_inv: float32 [3, 32, 256, 256], P(None, 'rows', 'cols'), may hold values from -1 to 3.1, as said below
- factor_tiles: float32 [2, 32, 8, 256, 256], P(None, 'rows', None, 'cols'), may hold values from -0.125 to 0.125
- tile_source: int32 [2, 32, 8], P(None, 'rows'), may hold values from 0 to 63, as said below
- tile_count: int32 [2, 32], P(None, 'rows'), may hold values from 1 to 8, as said below
Outputs:
- solution: float32 [3, 32, 256, 128], P(None, 'rows', 'cols')
The draws below stay inside these ranges and needn't reach their ends.
Inputs may be any that keep to these rules, and one draw needn't show every extreme that they name: `tile_source`: each source lies at a lower level than its target; supernode g mod 32 belongs to rows index (g mod 32) // 2, and that index differs from the target's by at most 7. The 8 sources of one supernode are distinct. `tile_count`: slots at or beyond the count hold no tile of the factor. At every target level some supernode has all 8 slots live. `diag_inv`: each block is lower triangular with a positive diagonal.
All inputs are finite; a program needn't handle non-finite values.
Results may differ from the reference program's by a relative error of at most 0.0003.
Values sent between devices are 32-bit elements; how exact they have to be, the bound alone decides.
No kernel may reach another device: no remote copies, remote signals or barrier semaphores. Data moves between devices by JAX's collectives and lax.ppermute only.
A program may use at most 64 MiB of HBM per device.

```python
import math
import jax
import jax.numpy as jnp
from jax import lax

B = 256
NRHS = 128
SUP_DEV = 2
LEV = 3
TPS = 8
KDEV = 7
NSUP = 32


def draw_diag_inv(key, part):
    key_off, key_diag = jax.random.split(key, 2)
    row_ids = jnp.arange(B, dtype=jnp.int32)[:, None]
    col_ids = jnp.arange(B, dtype=jnp.int32)[None, :]
    below = (col_ids < row_ids).astype(jnp.float32)
    identity = (col_ids == row_ids).astype(jnp.float32)
    spread = 0.6 / math.sqrt(B)
    off_diag = jax.random.normal(key_off, (LEV, NSUP, B, B), jnp.float32) * spread
    diagonal = jax.random.uniform(key_diag, (LEV, NSUP, B, 1), jnp.float32, 0.6, 1.4)
    return off_diag * below + diagonal * identity


def draw_tile_source(key, part):
    row_total = NSUP // SUP_DEV
    window_len = 2 * KDEV + 1
    cand_total = (LEV - 1) * window_len * SUP_DEV
    candidate = jnp.arange(cand_total, dtype=jnp.int32)
    cand_level = candidate // (window_len * SUP_DEV)
    cand_offset = candidate // SUP_DEV % window_len - KDEV
    cand_slot = candidate % SUP_DEV
    target_level = jnp.arange(1, LEV, dtype=jnp.int32)[:, None, None]
    target = jnp.arange(NSUP, dtype=jnp.int32)[None, :, None]
    device = target // SUP_DEV + cand_offset
    valid = (cand_level < target_level) & (device >= 0) & (device < row_total)
    noise = jax.random.randint(key, (LEV - 1, NSUP, cand_total), 0, 1 << 20)
    score = jnp.where(valid, noise * cand_total + candidate, (1 << 30) + candidate)
    corner = (target_level == LEV - 1) & (target == NSUP - 1) | (target_level == 1) & (target == 0)
    forced = (cand_level == target_level - 1) & (cand_offset == 0) & (cand_slot == target % SUP_DEV)
    score = jnp.where(corner & forced, -1, score)
    picked = jnp.argsort(score, axis=-1)[:, :, :TPS]
    chosen_device = target // SUP_DEV + cand_offset[picked]
    return (cand_level[picked] * NSUP + chosen_device * SUP_DEV + cand_slot[picked]).astype(jnp.int32)


def draw_tile_count(key, part):
    key_base, key_hot, key_pick = jax.random.split(key, 3)
    base = jax.random.randint(key_base, (LEV - 1, NSUP), 1, min(5, TPS + 1))
    hot = jax.random.randint(key_hot, (LEV - 1, NSUP), 0, 8) == 0
    chosen = jax.random.randint(key_pick, (LEV - 1, 1), 0, NSUP)
    filled = hot | (jnp.arange(NSUP, dtype=jnp.int32)[None, :] == chosen)
    return jnp.where(filled, TPS, base).astype(jnp.int32)


def shard_levels(key, shape, shards, low, largest):
    gain = 1.0
    for position, blocks in shards:
        heights = jax.random.uniform(jax.random.fold_in(jax.random.fold_in(key, 6), position), (blocks,), jnp.float32, low / len(shards), largest / len(shards))
        gain = gain * jnp.repeat(jnp.exp(heights), shape[position] // blocks).reshape((-1,) + (1,) * (len(shape) - 1 - position))
    return gain


def bell_draw(key, shape, width, bound, pieces=(), kind=jnp.bfloat16):
    values = jax.random.normal(key, shape, jnp.float32) * width
    if len(pieces) > 0:
        values = shard_levels(key, shape, pieces, -0.22, 0.18) * values
    return jnp.clip(values, min=-bound, max=bound).astype(kind)


def setup_inputs(seed: int = 0) -> dict:
    arg_keys = jax.random.split(jax.random.key(seed), 6)
    rhs = bell_draw(arg_keys[0], (LEV, NSUP, B, NRHS), 1.0, 6.0, ((1, 16), (2, 2)), jnp.float32)
    diag_inv = draw_diag_inv(jax.random.fold_in(arg_keys[5], 71), 0)
    factor_tiles = bell_draw(arg_keys[2], (LEV - 1, NSUP, TPS, B, B), (TPS * B) ** -0.5, 0.125, ((1, 16), (3, 2)), jnp.float32)
    tile_source = draw_tile_source(jax.random.fold_in(arg_keys[5], 71), 0)
    tile_count = draw_tile_count(jax.random.fold_in(arg_keys[5], 71), 0)
    return {"rhs": rhs, "diag_inv": diag_inv, "factor_tiles": factor_tiles, "tile_source": tile_source, "tile_count": tile_count}


def reference(rhs, diag_inv, factor_tiles, tile_source, tile_count):
    highest = lax.Precision.HIGHEST
    slot_ids = jnp.arange(TPS, dtype=jnp.int32)
    forward = jnp.zeros((LEV * NSUP, B, NRHS), jnp.float32)
    for height in range(LEV):
        if height > 0:
            def update_one(operands):
                tile_set, sources, live_count = operands
                live_rows = (slot_ids < live_count).astype(jnp.float32)
                picked = forward[sources] * live_rows[:, None, None]
                return jnp.einsum("kji,kjr->ir", tile_set, picked, precision=highest)

            update_sum = lax.map(update_one, (factor_tiles[height - 1], tile_source[height - 1], tile_count[height - 1]))
            residual = rhs[height] - update_sum
        else:
            residual = rhs[height]
        values = jnp.einsum("sij,sjr->sir", diag_inv[height], residual, precision=highest)
        forward = forward.at[height * NSUP:(height + 1) * NSUP].set(values)
    carried = jnp.zeros((LEV * NSUP, B, NRHS), jnp.float32)
    solution = jnp.zeros((LEV * NSUP, B, NRHS), jnp.float32)
    for height in reversed(range(LEV)):
        first_row = height * NSUP
        last_row = (height + 1) * NSUP
        residual = forward[first_row:last_row] - carried[first_row:last_row]
        values = jnp.einsum("sji,sjr->sir", diag_inv[height], residual, precision=highest)
        solution = solution.at[first_row:last_row].set(values)
        if height > 0:
            def spread_one(carry_sum, operands):
                tile_set, sources, live_count, own_values = operands
                live_rows = (slot_ids < live_count).astype(jnp.float32)
                term_set = jnp.einsum("kji,ir->kjr", tile_set, own_values, precision=highest) * live_rows[:, None, None]
                return carry_sum.at[sources].add(term_set), None

            carried, unused = lax.scan(spread_one, carried, (factor_tiles[height - 1], tile_source[height - 1], tile_count[height - 1], values))
    return solution.reshape(LEV, NSUP, B, NRHS)
```

```python
import functools

import jax
import jax.numpy as jnp
from jax import lax
from jax.experimental import pallas as pl
from jax.experimental.pallas import tpu as pltpu
from jax.sharding import PartitionSpec as P

KDEV = 7


def from_behind(value, axis, steps):
    count = lax.axis_size(axis)
    leading, last = (max(0, -steps), min(count, count - steps))
    return lax.ppermute(value, axis, [(source, source + steps) for source in range(leading, last)])


def local_any(rhs, diag_inv, factor_tiles, tile_source, tile_count):
    levels = rhs.shape[0]
    owned_count = rhs.shape[1]
    share_rows = rhs.shape[2]
    columns = rhs.shape[3]
    slot_count = tile_source.shape[2]
    reach_dev = KDEV
    window_len = 2 * reach_dev + 1
    total_sup = lax.axis_size("rows") * owned_count
    row_place = lax.axis_index("rows")
    highest = lax.Precision.HIGHEST
    slot_ids = jnp.arange(slot_count, dtype=jnp.int32)

    def window_places(sources):
        src_level = sources // total_sup
        within = sources % total_sup
        return (
            src_level * window_len + within // owned_count - row_place + reach_dev
        ) * owned_count + within % owned_count

    def live_mask(counts):
        return (slot_ids[None, :] < counts[:, None]).astype(jnp.float32)

    def full_rows(piece):
        return lax.all_gather(piece, "cols", axis=1, tiled=True)

    forward_values = []
    windows = []
    for height in range(levels):
        if height == 0:
            whole_block = full_rows(rhs[0])
        else:
            stacked = jnp.stack(windows, 0).reshape(
                height * window_len * owned_count, share_rows, columns
            )
            places = window_places(tile_source[height - 1])
            picked = (
                jnp.take(stacked, places, axis=0)
                * live_mask(tile_count[height - 1])[:, :, None, None]
            )
            partial_value = jnp.einsum(
                "skci,skcr->sir", factor_tiles[height - 1], picked, precision=highest
            )
            whole_block = full_rows(
                rhs[height]
                - lax.psum_scatter(partial_value, "cols", scatter_dimension=1, tiled=True)
            )
        values = jnp.einsum("sci,sir->scr", diag_inv[height], whole_block, precision=highest)
        forward_values.append(values)
        if height + 1 < levels:
            pieces = []
            for pull_offset in range(-reach_dev, reach_dev + 1):
                if pull_offset == 0:
                    pieces.append(values)
                else:
                    pieces.append(from_behind(values, "rows", -pull_offset))
            windows.append(jnp.stack(pieces, 0))
    carried = [jnp.zeros_like(forward_values[0]) for height in range(levels)]
    solution = [None] * levels
    for height in reversed(range(levels)):
        partial_value = jnp.einsum(
            "sci,scr->sir",
            diag_inv[height],
            forward_values[height] - carried[height],
            precision=highest,
        )
        own_share = lax.psum_scatter(partial_value, "cols", scatter_dimension=1, tiled=True)
        if height > 0:
            whole_block = lax.all_gather(own_share, "cols", axis=1, tiled=True)
        solution[height] = own_share
        if height > 0:
            term_set = jnp.einsum(
                "skci,sir->skcr", factor_tiles[height - 1], whole_block, precision=highest
            )
            term_set = term_set * live_mask(tile_count[height - 1])[:, :, None, None]
            places = window_places(tile_source[height - 1]).reshape(-1)
            targets = height * window_len * owned_count
            one_hot = (jnp.arange(targets, dtype=jnp.int32)[:, None] == places[None, :]).astype(
                jnp.float32
            )
            outgoing = jnp.einsum(
                "ms,slg->mlg",
                one_hot,
                term_set.reshape(owned_count * slot_count, share_rows, columns),
                precision=highest,
            )
            push_outgoing = outgoing.reshape(height, window_len, owned_count, share_rows, columns)
            received = push_outgoing[:, reach_dev]
            for offset in range(-reach_dev, reach_dev + 1):
                if offset != 0:
                    received = received + from_behind(
                        push_outgoing[:, reach_dev + offset], "rows", offset
                    )
            for lower_level in range(height):
                carried[lower_level] = carried[lower_level] + received[lower_level]
    return jnp.stack(solution, 0)


F32 = jnp.float32
BF16 = jnp.bfloat16
NN = (((1,), (0,)), ((), ()))
NT = (((1,), (1,)), ((), ()))
TN = (((0,), (0,)), ((), ()))
PIECES = 8


def halves(value):
    high = value.astype(BF16)
    return high, (value - high.astype(F32)).astype(BF16)


def dot3(left, right, dims):
    left_high, left_low = halves(left)
    right_high, right_low = halves(right)
    dot = functools.partial(lax.dot_general, dimension_numbers=dims, preferred_element_type=F32)
    return dot(left_high, right_high) + dot(left_low, right_high) + dot(left_high, right_low)


def ordered(mine, theirs, place, axis):
    first = jnp.where(place == 0, mine, theirs)
    second = jnp.where(place == 0, theirs, mine)
    return jnp.concatenate([first, second], axis)


def call(kernel, name, outs, args, scalars=1, scratch=()):
    in_specs = [pl.BlockSpec(memory_space=pltpu.SMEM)] * scalars
    in_specs += [pl.BlockSpec(memory_space=pltpu.VMEM)] * (len(args) - scalars)
    out_shape = [jax.ShapeDtypeStruct(shape, F32) for shape in outs]
    return pl.pallas_call(
        kernel,
        out_shape=out_shape,
        in_specs=in_specs,
        out_specs=[pl.BlockSpec(memory_space=pltpu.VMEM)] * len(outs),
        scratch_shapes=list(scratch),
        name=name,
        compiler_params=pltpu.CompilerParams(vmem_limit_bytes=40 * 1024 * 1024),
    )(*args)


def first_values(where, rhs_own, rhs_other, diag, mine, partner):
    core, col = where[0] % 2, where[1]
    half = mine.shape[1]
    for s in range(rhs_own.shape[0]):
        rows = ordered(rhs_own[s], rhs_other[s], col, 0)
        values = dot3(diag[s], rows, NN).T
        low, high = values[:half], values[half:]
        mine[s] = jnp.where(core == 0, low, high)
        partner[s] = jnp.where(core == 0, high, low)


def turned_rhs(where, rhs_own, rhs_other, mine, partner):
    core, col = where[0] % 2, where[1]
    half = mine.shape[2]
    for l in range(mine.shape[0]):
        for s in range(mine.shape[1]):
            rows = ordered(rhs_own[l, s].T, rhs_other[l, s].T, col, 1)
            low, high = rows[:half], rows[half:]
            mine[l, s] = jnp.where(core == 0, low, high)
            partner[l, s] = jnp.where(core == 0, high, low)


def tile_update(places, counts, *refs):
    tiles_own, tiles_partner = refs[:2]
    out, window = refs[-2:]
    pieces = refs[2:-2]
    sups = pieces[0].shape[0]
    for index, piece in enumerate(pieces):
        window[index * sups : (index + 1) * sups] = piece[...]
    slots, depth, width = tiles_own.shape[1:]
    for s in range(sups):
        tiles = tiles_own if s < sups // 2 else tiles_partner
        picked = []
        for k in range(slots):
            value = window[places[s * slots + k]]
            picked.append(jnp.where(k < counts[s], value, 0.0))
        left = jnp.concatenate(picked, 1)
        out[s] = dot3(left, tiles[s % (sups // 2)].reshape(slots * depth, width), NN)


def level_values(rhs, mine, theirs, d_own, d_partner, d_own_other, d_partner_other, own, other):
    sups = rhs.shape[0]
    for s in range(sups):
        residual = rhs[s] - (mine[s] + theirs[s])
        a, b = (d_own, d_own_other) if s < sups // 2 else (d_partner, d_partner_other)
        own[s] = dot3(residual, a[s % (sups // 2)], NT)
        other[s] = dot3(residual, b[s % (sups // 2)], NT)


def carry_products(places, counts, tiles_own, tiles_partner, totals, x, s):
    slots, depth, width = tiles_own.shape[1:]
    sups = totals.shape[0]
    half = counts.shape[0] // 2
    tiles = tiles_own if s < half else tiles_partner
    terms = dot3(x, tiles[s % half].reshape(slots * depth, width), NT)
    for k in range(slots):
        place = places[s * slots + k]
        term = terms[:, k * depth : (k + 1) * depth]
        totals[place] = totals[place] + jnp.where(k < counts[s], term, 0.0)


def top_carry(
    where, places, counts, rhs, mine, theirs, d_own, d_partner, d_own_other, d_partner_other,
    tiles_own, tiles_partner, solved_mine, solved_partner, lowest, *rest
):
    outs, totals = rest[:-1], rest[-1]
    col = where[1]
    sups = rhs.shape[0]
    half = sups // 2
    depth = tiles_own.shape[2]
    totals[...] = jnp.zeros_like(totals)
    for s in range(sups):
        a, b = (d_own, d_own_other) if s < half else (d_partner, d_partner_other)
        residual = rhs[s] - (mine[s] + theirs[s])
        own = dot3(residual, a[s % half], NT)
        other = dot3(residual, b[s % half], NT)
        x = dot3(own, a[s % half], NN) + dot3(other, b[s % half], NN)
        share = jnp.where(col == 0, x[:, :depth], x[:, depth:])
        if s < half:
            solved_mine[s] = share
        else:
            solved_partner[s % half] = share
        carry_products(places, counts, tiles_own, tiles_partner, totals, x, s)
    lowest[...] = totals[: lowest.shape[0]]
    for index, out in enumerate(outs):
        first = lowest.shape[0] + index * sups
        out[...] = totals[first : first + sups]


def middle_carry(
    where, places, counts, carried_own, carried_other, values_own, values_other,
    d_own, d_partner, d_own_other, d_partner_other,
    tiles_own, tiles_partner, lowest, solved_mine, solved_partner, *rest
):
    outs, totals = rest[:-1], rest[-1]
    col = where[1]
    sups = values_own.shape[0]
    half = sups // 2
    depth = tiles_own.shape[2]
    totals[...] = lowest[...]
    for s in range(sups):
        a, b = (d_own, d_own_other) if s < half else (d_partner, d_partner_other)
        own = values_own[s] - carried_own[s]
        other = values_other[s] - carried_other[s]
        x = dot3(own, a[s % half], NN) + dot3(other, b[s % half], NN)
        share = jnp.where(col == 0, x[:, :depth], x[:, depth:])
        if s < half:
            solved_mine[s] = share
        else:
            solved_partner[s % half] = share
        carry_products(places, counts, tiles_own, tiles_partner, totals, x, s)
    for index, out in enumerate(outs):
        out[...] = totals[index * sups : (index + 1) * sups]


def last_product(values, a, b, c, d, e, d_own, d_partner, mine, partner):
    sups = values.shape[0]
    half = sups // 2
    for s in range(sups):
        carried = a[s] + b[s] + c[s] + d[s] + e[s]
        diag, out = (d_own, mine) if s < half else (d_partner, partner)
        out[s % half] = dot3(values[s] - carried, diag[s % half], NN)


def turned_solution(where, mine, partner, own, other):
    core, col = where[0] % 2, where[1]
    depth = own.shape[1]
    for s in range(mine.shape[0]):
        both = ordered(mine[s], partner[s], core, 0)
        low, high = both[:, :depth].T, both[:, depth:].T
        own[s] = jnp.where(col == 0, low, high)
        other[s] = jnp.where(col == 0, high, low)


def turned_upper(where, mine2, partner2, mine1, partner1, out):
    core = where[0] % 2
    for s in range(mine2.shape[0]):
        out[0, s] = ordered(mine1[s], partner1[s], core, 0).T
        out[1, s] = ordered(mine2[s], partner2[s], core, 0).T


def local(rhs, diag_inv, factor_tiles, tile_source, tile_count):
    levels, owned, share_rows, columns = rhs.shape
    slots = tile_source.shape[2]
    sups = 2 * owned
    block = share_rows * 2
    half_columns = columns // 2
    row = lax.axis_index("rows")
    col = lax.axis_index("cols")
    where = jnp.stack([row, col]).astype(jnp.int32)
    rows_total = lax.axis_size("rows")
    total_sup = rows_total * owned
    piece = (sups, half_columns, share_rows)

    def swap_cols(value):
        return lax.ppermute(value, "cols", [(0, 1), (1, 0)])

    def swap_rows(value, bits):
        return lax.ppermute(value, "rows", [(r, r ^ bits) for r in range(rows_total)])

    def swap_core(value):
        return swap_rows(value, 1)

    def swap_x(value):
        return swap_rows(value, 2)

    def swap_far(value):
        inner = (rows_total // 4, 3 * rows_total // 4)
        return lax.ppermute(
            value, "rows",
            [(r, r ^ 12 if inner[0] <= r < inner[1] else r) for r in range(rows_total)],
        )

    def gather_pieces(value):
        far = swap_rows(value, 8)
        next_ = swap_rows(value, 4)
        mid = swap_far(value)
        beside = swap_x(value)
        return [
            value, beside, next_, swap_x(next_), far, swap_x(far), mid, swap_x(mid)
        ]

    def scatter_pieces(p):
        far = swap_rows(p[4] + swap_x(p[5]), 8)
        mid = swap_far(p[6] + swap_x(p[7]))
        next_ = swap_rows(p[2] + swap_x(p[3]), 4)
        beside = swap_x(p[1])
        return [p[0], beside, next_, far, mid]

    rhs_other = swap_cols(rhs[0])
    mine, partner = call(
        first_values, "first_values", [(owned, half_columns, share_rows)] * 2,
        [where, rhs[0], rhs_other, diag_inv[0]],
    )
    values0 = jnp.concatenate([mine, swap_core(partner)], 0)
    pieces0 = gather_pieces(values0)

    source = jnp.concatenate([tile_source, swap_core(tile_source)], 1)
    count = jnp.concatenate([tile_count, swap_core(tile_count)], 1)
    live = jnp.arange(slots, dtype=jnp.int32)[None, None, :] < count[:, :, None]
    within = source % total_sup
    place = (row ^ (within // owned)) * owned + within % owned
    place = place + source // total_sup * (PIECES * sups)
    places = jnp.where(live, place, 0).reshape(levels - 1, sups * slots)
    tiles_own = [factor_tiles[l] for l in range(levels - 1)]
    tiles_partner = [swap_core(tiles) for tiles in tiles_own]
    d_low_partner = swap_core(diag_inv[0])
    d_own = [diag_inv[l] for l in range(1, levels)]
    d_own_other = [swap_cols(d) for d in d_own]
    d_partner = [swap_core(d) for d in d_own]
    d_partner_other = [swap_core(d) for d in d_own_other]
    upper_other = swap_cols(rhs[1:])
    mine, partner = call(
        turned_rhs, "turned_rhs", [(levels - 1, owned, half_columns, block)] * 2,
        [where, rhs[1:], upper_other],
    )
    upper = jnp.concatenate([mine, swap_core(partner)], 1)

    def diag_args(l):
        return [d_own[l], d_partner[l], d_own_other[l], d_partner_other[l]]

    def update(l, pieces):
        return call(
            tile_update, "tile_update", [(sups, half_columns, block)],
            [places[l], count[l], tiles_own[l], tiles_partner[l], *pieces], 2,
            [pltpu.VMEM((len(pieces) * sups, half_columns, share_rows), F32)],
        )[0]

    partial = update(0, pieces0)
    values1, values1_other = call(
        level_values, "level_values", [piece] * 2,
        [upper[0], partial, swap_cols(partial), *diag_args(0)], 0,
    )
    pieces1 = gather_pieces(values1)

    partial = update(1, pieces0 + pieces1)
    window = PIECES * sups
    shared = (owned, half_columns, share_rows)
    mine2, partner2, lowest, *out = call(
        top_carry, "top_carry", [shared, shared, (window, half_columns, share_rows)] + [piece] * PIECES,
        [where, places[1], count[1], upper[1], partial, swap_cols(partial), *diag_args(1),
         tiles_own[1], tiles_partner[1]], 3,
        [pltpu.VMEM((2 * window, half_columns, share_rows), F32)],
    )
    partner2 = swap_core(partner2)
    carried = sum(scatter_pieces(out))

    mine1, partner1, *out = call(
        middle_carry, "middle_carry", [shared, shared] + [piece] * PIECES,
        [where, places[0], count[0], carried, swap_cols(carried), values1, values1_other,
         *diag_args(0), tiles_own[0], tiles_partner[0], lowest], 3,
        [pltpu.VMEM((window, half_columns, share_rows), F32)],
    )
    partner1 = swap_core(partner1)
    result_upper = call(
        turned_upper, "turned_upper", [(levels - 1, owned, share_rows, columns)],
        [where, mine2, partner2, mine1, partner1],
    )[0]
    mine, partner = call(
        last_product, "last_product", [(owned, half_columns, block)] * 2,
        [values0, *scatter_pieces(out), diag_inv[0], d_low_partner], 0,
    )
    own, other = call(
        turned_solution, "turned_solution", [(owned, share_rows, columns)] * 2,
        [where, mine, swap_core(partner)],
    )
    return jnp.concatenate([(own + swap_cols(other))[None], result_upper], 0)


def solution(mesh):
    placed = (
        P(None, "rows", "cols", None),
        P(None, "rows", "cols", None),
        P(None, "rows", None, "cols", None),
        P(None, "rows", None),
        P(None, "rows"),
    )
    small = mesh.shape["rows"] == 16 and mesh.shape["cols"] == 2
    return jax.shard_map(
        local if small else local_any,
        mesh=mesh,
        in_specs=placed,
        out_specs=P(None, "rows", "cols", None),
        check_vma=False,
    )
```

```python
import functools

import jax
import jax.numpy as jnp
from jax import lax
from jax.experimental import pallas as pl
from jax.experimental.pallas import tpu as pltpu
from jax.sharding import PartitionSpec as P

KDEV = 7


def from_behind(value, axis, steps):
    count = lax.axis_size(axis)
    leading, last = (max(0, -steps), min(count, count - steps))
    return lax.ppermute(value, axis, [(source, source + steps) for source in range(leading, last)])


def local_any(rhs, diag_inv, factor_tiles, tile_source, tile_count):
    levels = rhs.shape[0]
    owned_count = rhs.shape[1]
    share_rows = rhs.shape[2]
    columns = rhs.shape[3]
    slot_count = tile_source.shape[2]
    reach_dev = KDEV
    window_len = 2 * reach_dev + 1
    total_sup = lax.axis_size("rows") * owned_count
    row_place = lax.axis_index("rows")
    highest = lax.Precision.HIGHEST
    slot_ids = jnp.arange(slot_count, dtype=jnp.int32)

    def window_places(sources):
        src_level = sources // total_sup
        within = sources % total_sup
        return (
            src_level * window_len + within // owned_count - row_place + reach_dev
        ) * owned_count + within % owned_count

    def live_mask(counts):
        return (slot_ids[None, :] < counts[:, None]).astype(jnp.float32)

    def full_rows(piece):
        return lax.all_gather(piece, "cols", axis=1, tiled=True)

    forward_values = []
    windows = []
    for height in range(levels):
        if height == 0:
            whole_block = full_rows(rhs[0])
        else:
            stacked = jnp.stack(windows, 0).reshape(
                height * window_len * owned_count, share_rows, columns
            )
            places = window_places(tile_source[height - 1])
            picked = (
                jnp.take(stacked, places, axis=0)
                * live_mask(tile_count[height - 1])[:, :, None, None]
            )
            partial_value = jnp.einsum(
                "skci,skcr->sir", factor_tiles[height - 1], picked, precision=highest
            )
            whole_block = full_rows(
                rhs[height]
                - lax.psum_scatter(partial_value, "cols", scatter_dimension=1, tiled=True)
            )
        values = jnp.einsum("sci,sir->scr", diag_inv[height], whole_block, precision=highest)
        forward_values.append(values)
        if height + 1 < levels:
            pieces = []
            for pull_offset in range(-reach_dev, reach_dev + 1):
                if pull_offset == 0:
                    pieces.append(values)
                else:
                    pieces.append(from_behind(values, "rows", -pull_offset))
            windows.append(jnp.stack(pieces, 0))
    carried = [jnp.zeros_like(forward_values[0]) for height in range(levels)]
    solution = [None] * levels
    for height in reversed(range(levels)):
        partial_value = jnp.einsum(
            "sci,scr->sir",
            diag_inv[height],
            forward_values[height] - carried[height],
            precision=highest,
        )
        own_share = lax.psum_scatter(partial_value, "cols", scatter_dimension=1, tiled=True)
        if height > 0:
            whole_block = lax.all_gather(own_share, "cols", axis=1, tiled=True)
        solution[height] = own_share
        if height > 0:
            term_set = jnp.einsum(
                "skci,sir->skcr", factor_tiles[height - 1], whole_block, precision=highest
            )
            term_set = term_set * live_mask(tile_count[height - 1])[:, :, None, None]
            places = window_places(tile_source[height - 1]).reshape(-1)
            targets = height * window_len * owned_count
            one_hot = (jnp.arange(targets, dtype=jnp.int32)[:, None] == places[None, :]).astype(
                jnp.float32
            )
            outgoing = jnp.einsum(
                "ms,slg->mlg",
                one_hot,
                term_set.reshape(owned_count * slot_count, share_rows, columns),
                precision=highest,
            )
            push_outgoing = outgoing.reshape(height, window_len, owned_count, share_rows, columns)
            received = push_outgoing[:, reach_dev]
            for offset in range(-reach_dev, reach_dev + 1):
                if offset != 0:
                    received = received + from_behind(
                        push_outgoing[:, reach_dev + offset], "rows", offset
                    )
            for lower_level in range(height):
                carried[lower_level] = carried[lower_level] + received[lower_level]
    return jnp.stack(solution, 0)


F32 = jnp.float32
BF16 = jnp.bfloat16
NN = (((1,), (0,)), ((), ()))
NT = (((1,), (1,)), ((), ()))
PIECES = 8


def halves(value):
    high = value.astype(BF16)
    return high, (value - high.astype(F32)).astype(BF16)


def dot3(left, right, dims):
    left_high, left_low = halves(left)
    right_high, right_low = right if isinstance(right, tuple) else halves(right)
    dot = functools.partial(lax.dot_general, dimension_numbers=dims, preferred_element_type=F32)
    rows = left.shape[0]
    both = dot(jnp.concatenate([left_high, left_low], 0), right_high)
    return both[:rows] + both[rows:] + dot(left_high, right_low)


def ordered(mine, theirs, place, axis):
    first = jnp.where(place == 0, mine, theirs)
    second = jnp.where(place == 0, theirs, mine)
    return jnp.concatenate([first, second], axis)


def call(kernel, name, outs, args, scalars=1, scratch=()):
    in_specs = [pl.BlockSpec(memory_space=pltpu.SMEM)] * scalars
    in_specs += [pl.BlockSpec(memory_space=pltpu.VMEM)] * (len(args) - scalars)
    return pl.pallas_call(
        kernel,
        out_shape=[jax.ShapeDtypeStruct(shape, F32) for shape in outs],
        in_specs=in_specs,
        out_specs=[pl.BlockSpec(memory_space=pltpu.VMEM)] * len(outs),
        scratch_shapes=list(scratch),
        name=name,
        compiler_params=pltpu.CompilerParams(vmem_limit_bytes=VMEM_LIMIT),
    )(*args)


VMEM_LIMIT = 20 * 1024 * 1024


def split_kernel(own, partner, *outs):
    for tiles, high_out, low_out in ((own, outs[0], outs[1]), (partner, outs[2], outs[3])):
        high, low = halves(tiles[0, 0].reshape(high_out.shape[1:]))
        high_out[0] = high
        low_out[0] = low


def split_tiles(level, own, partner):
    owned, slots, depth, width = own.shape[1:]
    block_in = pl.BlockSpec((1, 1, slots, depth, width), lambda s: (level, s, 0, 0, 0))
    block_out = pl.BlockSpec((1, slots * depth, width), lambda s: (s, 0, 0))
    return pl.pallas_call(
        split_kernel,
        grid=(owned,),
        out_shape=[jax.ShapeDtypeStruct((owned, slots * depth, width), BF16)] * 4,
        in_specs=[block_in] * 2,
        out_specs=[block_out] * 4,
        name="split_tiles",
        compiler_params=pltpu.CompilerParams(vmem_limit_bytes=VMEM_LIMIT),
    )(own, partner)


def tile_of(tiles, s):
    half = tiles[0].shape[0]
    high, low = tiles[:2] if s < half else tiles[2:]
    return high[s % half], low[s % half]


def first_values(where, rhs_own, rhs_other, diag, mine, partner):
    core, col = where[0] % 2, where[1]
    half = mine.shape[1]
    for s in range(rhs_own.shape[0]):
        rows = ordered(rhs_own[s], rhs_other[s], col, 0)
        values = dot3(diag[0, s], rows, NN).T
        low, high = values[:half], values[half:]
        mine[s] = jnp.where(core == 0, low, high)
        partner[s] = jnp.where(core == 0, high, low)


def turned_rhs(where, rhs_own, rhs_other, mine, partner):
    core, col = where[0] % 2, where[1]
    half = mine.shape[2]
    for l in range(mine.shape[0]):
        for s in range(mine.shape[1]):
            rows = ordered(rhs_own[l, s].T, rhs_other[l, s].T, col, 1)
            low, high = rows[:half], rows[half:]
            mine[l, s] = jnp.where(core == 0, low, high)
            partner[l, s] = jnp.where(core == 0, high, low)


def tile_update(index, based, places, *refs):
    tiles, refs = refs[:4], refs[4:]
    if based:
        base, refs = refs[0], refs[1:]
    out, window = refs[-2:]
    pieces = refs[:-2]
    sups = pieces[0].shape[0]
    for number, piece in enumerate(pieces):
        window[number * sups : (number + 1) * sups] = piece[...]
    slots = places.shape[1] // sups
    for s in range(sups):
        picked = []
        for k in range(slots):
            place = places[index, s * slots + k]
            value = window[jnp.maximum(place, 0)]
            picked.append(jnp.where(place >= 0, value, 0.0))
        total = dot3(jnp.concatenate(picked, 1), tile_of(tiles, s), NN)
        out[s] = total + base[s] if based else total


def diag_of(level, diags, s):
    own, partner, own_other, partner_other = diags
    half = own.shape[1]
    if s < half:
        return own[level, s], own_other[level - 1, s]
    return partner[level, s % half], partner_other[level - 1, s % half]


def upper_of(level, mine, partner, s):
    half = mine.shape[1]
    return mine[level - 1, s] if s < half else partner[level - 1, s % half]


def level_values(level, rhs, rhs_partner, mine, theirs, d0, d1, d2, d3, own, other):
    for s in range(own.shape[0]):
        residual = upper_of(level, rhs, rhs_partner, s) - (mine[s] + theirs[s])
        diag, diag_other = diag_of(level, (d0, d1, d2, d3), s)
        own[s] = dot3(residual, diag, NT)
        other[s] = dot3(residual, diag_other, NT)


def add_terms(index, places, tiles, x, s, totals, depth):
    terms = dot3(x, tile_of(tiles, s), NT)
    slots = terms.shape[1] // depth
    for k in range(slots):
        place = places[index, s * slots + k]
        term = jnp.where(place >= 0, terms[:, k * depth : (k + 1) * depth], 0.0)
        place = jnp.maximum(place, 0)
        totals[place] = totals[place] + term


def share_out(col, x, s, solved_mine, solved_partner):
    depth = solved_mine.shape[2]
    half = solved_mine.shape[0]
    share = jnp.where(col == 0, x[:, :depth], x[:, depth:])
    if s < half:
        solved_mine[s] = share
    else:
        solved_partner[s % half] = share


def pieces_out(totals, outs):
    sups = outs[0].shape[0]
    for number, out in enumerate(outs):
        out[...] = totals[number * sups : (number + 1) * sups]


def top_carry(
    level, where, places, rhs, rhs_partner, mine, theirs, d0, d1, d2, d3, t0, t1, t2, t3,
    solved_mine, solved_partner, solved, *rest
):
    outs, totals = rest[:-1], rest[-1]
    totals[...] = jnp.zeros_like(totals)
    for s in range(solved.shape[0]):
        residual = upper_of(level, rhs, rhs_partner, s) - (mine[s] + theirs[s])
        diag, diag_other = diag_of(level, (d0, d1, d2, d3), s)
        own = dot3(residual, diag, NT)
        other = dot3(residual, diag_other, NT)
        x = dot3(own, diag, NN) + dot3(other, diag_other, NN)
        solved[s] = x
        share_out(where[1], x, s, solved_mine, solved_partner)
        add_terms(2, places, (t0, t1, t2, t3), x, s, totals, outs[0].shape[2])
    pieces_out(totals, outs)


def lowest_carry(places, solved, t0, t1, t2, t3, totals):
    totals[...] = jnp.zeros_like(totals)
    for s in range(solved.shape[0]):
        add_terms(1, places, (t0, t1, t2, t3), solved[s], s, totals, totals.shape[2])


def middle_carry(
    level, where, places, carried_own, carried_other, values_own, values_other,
    d0, d1, d2, d3, t0, t1, t2, t3, lowest, solved_mine, solved_partner, *rest
):
    outs, totals = rest[:-1], rest[-1]
    totals[...] = lowest[...]
    for s in range(values_own.shape[0]):
        diag, diag_other = diag_of(level, (d0, d1, d2, d3), s)
        own = values_own[s] - carried_own[s]
        other = values_other[s] - carried_other[s]
        x = dot3(own, diag, NN) + dot3(other, diag_other, NN)
        share_out(where[1], x, s, solved_mine, solved_partner)
        add_terms(0, places, (t0, t1, t2, t3), x, s, totals, outs[0].shape[2])
    pieces_out(totals, outs)


def last_product(values, a, b, c, d, e, d_own, d_partner, mine, partner):
    sups = values.shape[0]
    half = sups // 2
    for s in range(sups):
        carried = a[s] + b[s] + c[s] + d[s] + e[s]
        diag, out = (d_own, mine) if s < half else (d_partner, partner)
        out[s % half] = dot3(values[s] - carried, diag[0, s % half], NN)


def turned_solution(where, mine, partner, own, other):
    core, col = where[0] % 2, where[1]
    depth = own.shape[1]
    for s in range(mine.shape[0]):
        both = ordered(mine[s], partner[s], core, 0)
        low, high = both[:, :depth].T, both[:, depth:].T
        own[s] = jnp.where(col == 0, low, high)
        other[s] = jnp.where(col == 0, high, low)


def turned_upper(where, mine2, partner2, mine1, partner1, out):
    core = where[0] % 2
    for s in range(mine2.shape[0]):
        out[0, s] = ordered(mine1[s], partner1[s], core, 0).T
        out[1, s] = ordered(mine2[s], partner2[s], core, 0).T


def local(rhs, diag_inv, factor_tiles, tile_source, tile_count):
    levels, owned, share_rows, columns = rhs.shape
    slots = tile_source.shape[2]
    sups = 2 * owned
    block = share_rows * 2
    half_columns = columns // 2
    row = lax.axis_index("rows")
    col = lax.axis_index("cols")
    where = jnp.stack([row, col]).astype(jnp.int32)
    rows_total = lax.axis_size("rows")
    total_sup = rows_total * owned
    piece = (sups, half_columns, share_rows)
    shared = (owned, half_columns, share_rows)
    window = (PIECES * sups, half_columns, share_rows)
    after = lax.optimization_barrier

    def swap_cols(value):
        return lax.ppermute(value, "cols", [(0, 1), (1, 0)])

    def swap_rows(value, bits):
        return lax.ppermute(value, "rows", [(r, r ^ bits) for r in range(rows_total)])

    def swap_core(value):
        return swap_rows(value, 1)

    def swap_x(value):
        return swap_rows(value, 2)

    def swap_mid(value):
        low, high = rows_total // 4, 3 * rows_total // 4
        pairs = [(r, r ^ 12 if low <= r < high else r) for r in range(rows_total)]
        return lax.ppermute(value, "rows", pairs)

    def gather_pieces(value):
        far = swap_rows(value, 8)
        mid = swap_mid(value)
        near = swap_rows(value, 4)
        beside = swap_x(value)
        return [value, beside, near, swap_x(near), far, swap_x(far), mid, swap_x(mid)]

    def scatter_pieces(p):
        far = swap_rows(p[4] + swap_x(p[5]), 8)
        mid = swap_mid(p[6] + swap_x(p[7]))
        near = swap_rows(p[2] + swap_x(p[3]), 4)
        beside = swap_x(p[1])
        return [p[0], beside, near, far, mid]

    rhs0 = rhs[0]
    rhs0_other = swap_cols(rhs0)
    upper_own, d_own, rhs0 = after((rhs[1:], diag_inv[1:], rhs0))
    d_own_other = swap_cols(d_own)
    upper_other = swap_cols(upper_own)
    tiles_partner = swap_core(factor_tiles)
    d_partner = swap_core(diag_inv)
    source_partner = swap_core(tile_source)
    count_partner = swap_core(tile_count)
    mine, partner = call(
        first_values, "first_values", [shared] * 2, [where, rhs0, rhs0_other, diag_inv]
    )
    values0 = jnp.concatenate([mine, swap_core(partner)], 0)
    pieces0 = gather_pieces(values0)

    source = jnp.concatenate([tile_source, source_partner], 1)
    count = jnp.concatenate([tile_count, count_partner], 1)
    live = jnp.arange(slots, dtype=jnp.int32)[None, None, :] < count[:, :, None]
    within = source % total_sup
    place = (row ^ (within // owned)) * owned + within % owned
    lower = source // total_sup
    places = jnp.stack(
        [
            jnp.where(live[0], place[0], -1),
            jnp.where(live[1] & (lower[1] == 0), place[1], -1),
            jnp.where(live[1] & (lower[1] == 1), place[1], -1),
        ]
    ).reshape(3, sups * slots)
    tiles = [split_tiles(l, factor_tiles, tiles_partner) for l in range(levels - 1)]
    d_partner_other = swap_core(d_own_other)
    diags = [diag_inv, d_partner, d_own_other, d_partner_other]
    upper, partner = call(
        turned_rhs, "turned_rhs", [(levels - 1, owned, half_columns, block)] * 2,
        [where, upper_own, upper_other],
    )
    upper_partner = swap_core(partner)

    def update(name, index, l, pieces, base=()):
        return call(
            functools.partial(tile_update, index, len(base) > 0), name,
            [(sups, half_columns, block)],
            [places, *tiles[l], *base, *pieces], 1, [pltpu.VMEM(window, F32)],
        )[0]

    partial = update("update_middle", 0, 0, pieces0)
    values1, values1_other = call(
        functools.partial(level_values, 1), "level_values", [piece] * 2,
        [upper, upper_partner, partial, swap_cols(partial), *diags], 0,
    )
    pieces1 = gather_pieces(values1)
    base = update("update_top_low", 1, 1, pieces0)

    partial = update("update_top", 2, 1, pieces1, [base])
    mine2, partner2, solved, *out = call(
        functools.partial(top_carry, 2), "top_carry",
        [shared, shared, (sups, half_columns, block)] + [piece] * PIECES,
        [where, places, upper, upper_partner, partial, swap_cols(partial), *diags, *tiles[1]], 2,
        [pltpu.VMEM(window, F32)],
    )
    carried = sum(scatter_pieces(out))
    lowest = call(lowest_carry, "lowest_carry", [window], [places, solved, *tiles[1]])[0]
    partner2 = swap_core(partner2)

    mine1, partner1, *out = call(
        functools.partial(middle_carry, 1), "middle_carry", [shared, shared] + [piece] * PIECES,
        [where, places, carried, swap_cols(carried), values1, values1_other, *diags,
         *tiles[0], lowest], 2,
        [pltpu.VMEM(window, F32)],
    )
    partner1 = swap_core(partner1)
    result_upper = call(
        turned_upper, "turned_upper", [(levels - 1, owned, share_rows, columns)],
        [where, mine2, partner2, mine1, partner1],
    )[0]

    mine, partner = call(
        last_product, "last_product", [(owned, half_columns, block)] * 2,
        [values0, *scatter_pieces(out), diag_inv, d_partner], 0,
    )
    own, other = call(
        turned_solution, "turned_solution", [(owned, share_rows, columns)] * 2,
        [where, mine, swap_core(partner)],
    )
    return jnp.concatenate([(own + swap_cols(other))[None], result_upper], 0)


def solution(mesh):
    placed = (
        P(None, "rows", "cols", None),
        P(None, "rows", "cols", None),
        P(None, "rows", None, "cols", None),
        P(None, "rows", None),
        P(None, "rows"),
    )
    small = mesh.shape["rows"] == 16 and mesh.shape["cols"] == 2
    return jax.shard_map(
        local if small else local_any,
        mesh=mesh,
        in_specs=placed,
        out_specs=P(None, "rows", "cols", None),
        check_vma=False,
    )
```

```python
import functools

import jax
import jax.numpy as jnp
from jax import lax
from jax.experimental import pallas as pl
from jax.experimental.pallas import tpu as pltpu
from jax.sharding import PartitionSpec as P

KDEV = 7


def from_behind(value, axis, steps):
    count = lax.axis_size(axis)
    leading, last = (max(0, -steps), min(count, count - steps))
    return lax.ppermute(value, axis, [(source, source + steps) for source in range(leading, last)])


def local_any(rhs, diag_inv, factor_tiles, tile_source, tile_count):
    levels = rhs.shape[0]
    owned_count = rhs.shape[1]
    share_rows = rhs.shape[2]
    columns = rhs.shape[3]
    slot_count = tile_source.shape[2]
    reach_dev = KDEV
    window_len = 2 * reach_dev + 1
    total_sup = lax.axis_size("rows") * owned_count
    row_place = lax.axis_index("rows")
    highest = lax.Precision.HIGHEST
    slot_ids = jnp.arange(slot_count, dtype=jnp.int32)

    def window_places(sources):
        src_level = sources // total_sup
        within = sources % total_sup
        return (
            src_level * window_len + within // owned_count - row_place + reach_dev
        ) * owned_count + within % owned_count

    def live_mask(counts):
        return (slot_ids[None, :] < counts[:, None]).astype(jnp.float32)

    def full_rows(piece):
        return lax.all_gather(piece, "cols", axis=1, tiled=True)

    forward_values = []
    windows = []
    for height in range(levels):
        if height == 0:
            whole_block = full_rows(rhs[0])
        else:
            stacked = jnp.stack(windows, 0).reshape(
                height * window_len * owned_count, share_rows, columns
            )
            places = window_places(tile_source[height - 1])
            picked = (
                jnp.take(stacked, places, axis=0)
                * live_mask(tile_count[height - 1])[:, :, None, None]
            )
            partial_value = jnp.einsum(
                "skci,skcr->sir", factor_tiles[height - 1], picked, precision=highest
            )
            whole_block = full_rows(
                rhs[height]
                - lax.psum_scatter(partial_value, "cols", scatter_dimension=1, tiled=True)
            )
        values = jnp.einsum("sci,sir->scr", diag_inv[height], whole_block, precision=highest)
        forward_values.append(values)
        if height + 1 < levels:
            pieces = []
            for pull_offset in range(-reach_dev, reach_dev + 1):
                if pull_offset == 0:
                    pieces.append(values)
                else:
                    pieces.append(from_behind(values, "rows", -pull_offset))
            windows.append(jnp.stack(pieces, 0))
    carried = [jnp.zeros_like(forward_values[0]) for height in range(levels)]
    solution = [None] * levels
    for height in reversed(range(levels)):
        partial_value = jnp.einsum(
            "sci,scr->sir",
            diag_inv[height],
            forward_values[height] - carried[height],
            precision=highest,
        )
        own_share = lax.psum_scatter(partial_value, "cols", scatter_dimension=1, tiled=True)
        if height > 0:
            whole_block = lax.all_gather(own_share, "cols", axis=1, tiled=True)
        solution[height] = own_share
        if height > 0:
            term_set = jnp.einsum(
                "skci,sir->skcr", factor_tiles[height - 1], whole_block, precision=highest
            )
            term_set = term_set * live_mask(tile_count[height - 1])[:, :, None, None]
            places = window_places(tile_source[height - 1]).reshape(-1)
            targets = height * window_len * owned_count
            one_hot = (jnp.arange(targets, dtype=jnp.int32)[:, None] == places[None, :]).astype(
                jnp.float32
            )
            outgoing = jnp.einsum(
                "ms,slg->mlg",
                one_hot,
                term_set.reshape(owned_count * slot_count, share_rows, columns),
                precision=highest,
            )
            push_outgoing = outgoing.reshape(height, window_len, owned_count, share_rows, columns)
            received = push_outgoing[:, reach_dev]
            for offset in range(-reach_dev, reach_dev + 1):
                if offset != 0:
                    received = received + from_behind(
                        push_outgoing[:, reach_dev + offset], "rows", offset
                    )
            for lower_level in range(height):
                carried[lower_level] = carried[lower_level] + received[lower_level]
    return jnp.stack(solution, 0)


F32 = jnp.float32
BF16 = jnp.bfloat16
NN = (((1,), (0,)), ((), ()))
NT = (((1,), (1,)), ((), ()))
PIECES = 8


def halves(value):
    high = value.astype(BF16)
    return high, (value - high.astype(F32)).astype(BF16)


def dot3(left, right, dims):
    left_high, left_low = halves(left)
    right_high, right_low = right if isinstance(right, tuple) else halves(right)
    dot = functools.partial(lax.dot_general, dimension_numbers=dims, preferred_element_type=F32)
    rows = left.shape[0]
    both = dot(jnp.concatenate([left_high, left_low], 0), right_high)
    return both[:rows] + both[rows:] + dot(left_high, right_low)


def ordered(mine, theirs, place, axis):
    first = jnp.where(place == 0, mine, theirs)
    second = jnp.where(place == 0, theirs, mine)
    return jnp.concatenate([first, second], axis)


VMEM_LIMIT = 20 * 1024 * 1024


def options(cost):
    return dict(
        cost_estimate=pl.CostEstimate(flops=cost * 1000000, bytes_accessed=0, transcendentals=0),
        compiler_params=pltpu.CompilerParams(vmem_limit_bytes=VMEM_LIMIT),
    )


def call(kernel, name, outs, args, scalars=1, scratch=(), cost=1000):
    in_specs = [pl.BlockSpec(memory_space=pltpu.SMEM)] * scalars
    in_specs += [pl.BlockSpec(memory_space=pltpu.VMEM)] * (len(args) - scalars)
    return pl.pallas_call(
        kernel,
        out_shape=[jax.ShapeDtypeStruct(shape, F32) for shape in outs],
        in_specs=in_specs,
        out_specs=[pl.BlockSpec(memory_space=pltpu.VMEM)] * len(outs),
        scratch_shapes=list(scratch),
        name=name,
        **options(cost),
    )(*args)


def prepare(kernel, name, level, own, partner, diags, outs, cost):
    own = pltpu.with_memory_space_constraint(own, pltpu.HBM)
    owned, slots, depth, width = own.shape[1:]
    block_in = pl.BlockSpec((1, 1, slots, depth, width), lambda s: (level, s, 0, 0, 0))
    diag_in = [pl.BlockSpec((1, 1) + d.shape[2:], lambda s, at=at: (at, s, 0, 0))
               for d, at in zip(diags, (level + 1, level + 1, level, level))]
    return pl.pallas_call(
        kernel,
        grid=(owned,),
        out_shape=[jax.ShapeDtypeStruct((owned,) + shape, kind) for shape, kind in outs * 2],
        in_specs=[block_in] * 2 + diag_in,
        out_specs=[pl.BlockSpec((1,) + shape, lambda s: (s, 0, 0)) for shape, _ in outs * 2],
        name=name,
        **options(cost),
    )(own, partner, *diags)


def put_halves(value, high_out, low_out):
    high, low = halves(value)
    high_out[0] = high
    low_out[0] = low


def flat(tiles):
    return tiles[0, 0].reshape(-1, tiles.shape[-1])


def split_tiles(own, partner, *outs):
    put_halves(flat(own), *outs[:2])
    put_halves(flat(partner), *outs[2:])


def both(diag, diag_other):
    return jnp.concatenate([diag[0, 0], diag_other[0, 0]], 0)


def diag_by_tiles(own, partner, d0, d1, d2, d3, *outs):
    put_halves(dot3(both(d0, d2), flat(own), NT), *outs[:2])
    put_halves(dot3(both(d1, d3), flat(partner), NT), *outs[2:])


def gram_by_tiles(own, partner, d0, d1, d2, d3, *outs):
    for tiles, diag, out in ((own, both(d0, d2), outs[:3]), (partner, both(d1, d3), outs[3:])):
        gram = dot3(diag.T, diag, NN)
        put_halves(dot3(gram, flat(tiles), NT), *out[:2])
        out[2][0] = gram


def part_of(parts, s):
    count = len(parts) // 2
    half = parts[0].shape[0]
    chosen = parts[:count] if s < half else parts[count:]
    return tuple(part[s % half] for part in chosen)


def first_values(rhs_own, rhs_other, diag, mine, partner):
    core, col = lax.axis_index("rows") % 2, lax.axis_index("cols")
    half = mine.shape[1]
    for s in range(rhs_own.shape[0]):
        rows = ordered(rhs_own[s], rhs_other[s], col, 0)
        values = dot3(diag[0, s], rows, NN).T
        low, high = values[:half], values[half:]
        mine[s] = jnp.where(core == 0, low, high)
        partner[s] = jnp.where(core == 0, high, low)


def first_call(rhs_own, rhs_other, diag):
    owned, depth, columns = rhs_own.shape
    whole = pl.BlockSpec((owned, depth, columns), lambda i: (0, 0, 0))
    half = pl.BlockSpec((owned, columns // 2, depth), lambda i: (0, 0, 0))
    return pl.pallas_call(
        first_values,
        grid=(1,),
        out_shape=[jax.ShapeDtypeStruct((owned, columns // 2, depth), F32)] * 2,
        in_specs=[
            whole, whole,
            pl.BlockSpec((1,) + diag.shape[1:], lambda i: (0, 0, 0, 0)),
        ],
        out_specs=[half, half],
        name="first_values",
        **options(500),
    )(rhs_own, rhs_other, pltpu.with_memory_space_constraint(diag, pltpu.HBM))


def slot_places(sources, counts, places):
    row = lax.axis_index("rows")
    levels, owned, slots = sources.shape
    total = lax.axis_size("rows") * owned
    for l in range(levels):
        for s in range(owned):
            for k in range(slots):
                source = sources[l, s, k]
                live = k < counts[l, s]
                lower = jnp.where(source >= total, 1, 0)
                within = source - lower * total
                place = (row ^ (within // owned)) * owned + within % owned
                at = s * slots + k
                if l == 0:
                    places[0, at] = jnp.where(live, place, -1)
                else:
                    places[1, at] = jnp.where(live & (lower == 0), place, -1)
                    places[2, at] = jnp.where(live & (lower == 1), place, -1)


def place_of(places, index, slot, owned):
    own, partner = places
    count = own.shape[1]
    if slot < count:
        place = own[index, slot]
        return jnp.maximum(place, 0), place >= 0
    place = partner[index, slot - count]
    return jnp.where(place >= 0, place ^ owned, 0), place >= 0


def turned_rhs(rhs, mine, partner):
    core = lax.axis_index("rows") % 2
    half = mine.shape[2]
    for l in range(mine.shape[0]):
        for s in range(mine.shape[1]):
            rows = rhs[l + 1, s].T
            low, high = rows[:half], rows[half:]
            mine[l, s] = jnp.where(core == 0, low, high)
            partner[l, s] = jnp.where(core == 0, high, low)


def gathered(index, places, pieces, window):
    sups = pieces[0].shape[0]
    slots = 2 * places[0].shape[1] // sups
    for number, piece in enumerate(pieces):
        window[number * sups : (number + 1) * sups] = piece[...]
    for s in range(sups):
        picked = []
        for k in range(slots):
            place, live = place_of(places, index, s * slots + k, sups // 2)
            picked.append(jnp.where(live, window[place], 0.0))
        yield jnp.concatenate(picked, 1)


def upper_of(level, mine, partner, s):
    half = mine.shape[1]
    return mine[level - 1, s] if s < half else partner[level - 1, s % half]


def update_lower(index, level, places, places_partner, rhs, rhs_partner, *refs):
    tiles, pieces, (out, window) = refs[:4], refs[4:-2], refs[-2:]
    col = lax.axis_index("cols")
    for s, left in enumerate(gathered(index, (places, places_partner), pieces, window)):
        right = upper_of(level, rhs, rhs_partner, s)
        zero = jnp.zeros_like(right)
        base = jnp.concatenate([jnp.where(col == 0, right, zero), jnp.where(col == 0, zero, right)], 1)
        out[s] = base - dot3(left, part_of(tiles, s), NN)


def level_values(mine, theirs, d0, d1, residual, values):
    half = d0.shape[1]
    for s in range(residual.shape[0]):
        left = mine[s] + theirs[s]
        residual[s] = left
        values[s] = dot3(left, d0[1, s] if s < half else d1[1, s % half], NT)


def update_top(places, places_partner, *refs):
    tiles, base, pieces, (out, window) = refs[:4], refs[4], refs[5:-2], refs[-2:]
    for s, left in enumerate(gathered(2, (places, places_partner), pieces, window)):
        out[s] = base[s] - dot3(left, part_of(tiles, s), NN)


def add_terms(index, places, tiles, left, s, totals):
    owned = tiles[0].shape[0]
    depth = totals.shape[2]
    terms = dot3(left, part_of(tiles, s), NN)
    slots = terms.shape[1] // depth
    for k in range(slots):
        place, live = place_of(places, index, s * slots + k, owned)
        term = jnp.where(live, terms[:, k * depth : (k + 1) * depth], 0.0)
        totals[place] = totals[place] + term


def share_out(col, x, s, solved_mine, solved_partner):
    depth = solved_mine.shape[2]
    half = solved_mine.shape[0]
    share = jnp.where(col == 0, x[:, :depth], x[:, depth:])
    if s < half:
        solved_mine[s] = share
    else:
        solved_partner[s % half] = share


def pieces_out(totals, outs):
    sups = outs[0].shape[0]
    for number, out in enumerate(outs):
        out[...] = totals[number * sups : (number + 1) * sups]


def top_carry(places, places_partner, mine, theirs, t0, t1, t2, t3, residual, *rest):
    outs, totals = rest[:-1], rest[-1]
    totals[...] = jnp.zeros_like(totals)
    for s in range(residual.shape[0]):
        left = mine[s] + theirs[s]
        residual[s] = left
        add_terms(2, (places, places_partner), (t0, t1, t2, t3), left, s, totals)
    pieces_out(totals, outs)


def lowest_carry(
    places, places_partner, residual, t0, t1, t2, t3, g0, g1, middle, d2, d3,
    totals, solved_mine, solved_partner, other,
):
    totals[...] = jnp.zeros_like(totals)
    half = g0.shape[0]
    col = lax.axis_index("cols")
    for s in range(residual.shape[0]):
        gram, diag = (g0[s], d2[0, s]) if s < half else (g1[s % half], d3[0, s % half])
        share_out(col, dot3(residual[s], gram, NN), s, solved_mine, solved_partner)
        add_terms(1, (places, places_partner), (t0, t1, t2, t3), residual[s], s, totals)
        other[s] = dot3(middle[s], diag, NT)


def middle_carry(
    places, places_partner, carried_own, carried_other, values_own, values_other, t0, t1, t2, t3, lowest,
    residual, *rest
):
    outs, totals = rest[:-1], rest[-1]
    totals[...] = lowest[...]
    for s in range(values_own.shape[0]):
        left = jnp.concatenate(
            [values_own[s] - carried_own[s], values_other[s] - carried_other[s]], 1
        )
        residual[s] = left
        add_terms(0, (places, places_partner), (t0, t1, t2, t3), left, s, totals)
    pieces_out(totals, outs)


def middle_solved(residual, d0, d1, d2, d3, solved_mine, solved_partner):
    depth = solved_mine.shape[2]
    half = d0.shape[1]
    for s in range(residual.shape[0]):
        diag, diag_other = (d0[1, s], d2[0, s]) if s < half else (d1[1, s % half], d3[0, s % half])
        left = residual[s]
        x = dot3(left[:, :depth], diag, NN) + dot3(left[:, depth:], diag_other, NN)
        share_out(lax.axis_index("cols"), x, s, solved_mine, solved_partner)


def last_product(values, a, b, c, d, e, d_own, d_partner, mine, partner):
    sups = values.shape[0]
    half = sups // 2
    for s in range(sups):
        carried = a[s] + b[s] + c[s] + d[s] + e[s]
        diag, out = (d_own, mine) if s < half else (d_partner, partner)
        out[s % half] = dot3(values[s] - carried, diag[0, s % half], NN)


def turned_solution(mine, partner, own, other):
    core, col = lax.axis_index("rows") % 2, lax.axis_index("cols")
    depth = own.shape[1]
    for s in range(mine.shape[0]):
        both = ordered(mine[s], partner[s], core, 0)
        low, high = both[:, :depth].T, both[:, depth:].T
        own[s] = jnp.where(col == 0, low, high)
        other[s] = jnp.where(col == 0, high, low)


def turned_upper(mine2, partner2, mine1, partner1, out):
    core = lax.axis_index("rows") % 2
    for s in range(mine2.shape[0]):
        out[0, s] = ordered(mine1[s], partner1[s], core, 0).T
        out[1, s] = ordered(mine2[s], partner2[s], core, 0).T


def local(rhs, diag_inv, factor_tiles, tile_source, tile_count):
    levels, owned, share_rows, columns = rhs.shape
    slots = tile_source.shape[2]
    sups = 2 * owned
    block = share_rows * 2
    half_columns = columns // 2
    rows_total = lax.axis_size("rows")
    piece = (sups, half_columns, share_rows)
    shared = (owned, half_columns, share_rows)
    window = (PIECES * sups, half_columns, share_rows)
    after = lax.optimization_barrier

    def swap_cols(value):
        return lax.ppermute(value, "cols", [(0, 1), (1, 0)])

    def swap_rows(value, bits):
        return lax.ppermute(value, "rows", [(r, r ^ bits) for r in range(rows_total)])

    def swap_core(value):
        return swap_rows(value, 1)

    def swap_x(value):
        return swap_rows(value, 2)

    def swap_mid(value):
        low, high = rows_total // 4, 3 * rows_total // 4
        pairs = [(r, r ^ 12 if low <= r < high else r) for r in range(rows_total)]
        return lax.ppermute(value, "rows", pairs)

    def gather_pieces(value):
        far = swap_rows(value, 8)
        beside = swap_x(value)
        mid = swap_mid(value)
        near = swap_rows(value, 4)
        return [
            value, beside, near, swap_x(near), far, swap_x(far), mid, swap_mid(beside)
        ]

    def scatter_pieces(p):
        far = swap_rows(p[4] + swap_x(p[5]), 8)
        mid = swap_mid(p[6] + swap_x(p[7]))
        near = swap_rows(p[2] + swap_x(p[3]), 4)
        return [p[0], far, mid, near, swap_x(p[1])]

    rhs0 = rhs[0]
    rhs0_other = swap_cols(rhs0)
    tiles_partner = swap_core(factor_tiles)
    d_partner = swap_core(diag_inv)
    own_places = pl.pallas_call(
        slot_places,
        out_shape=jax.ShapeDtypeStruct((levels, owned * slots), jnp.int32),
        in_specs=[pl.BlockSpec(memory_space=pltpu.SMEM)] * 2,
        out_specs=pl.BlockSpec(memory_space=pltpu.SMEM),
        name="slot_places",
        **options(500),
    )(tile_source, tile_count)
    places = [own_places, swap_core(own_places)]
    diag, rhs0 = after((diag_inv, rhs0))
    d_other = swap_cols(diag[1:])
    rhs0, places, tiles_partner, d_partner = after((rhs0, places, tiles_partner, d_partner))
    mine, partner = first_call(rhs0, rhs0_other, diag_inv)
    values0 = jnp.concatenate([mine, swap_core(partner)], 0)
    pieces0 = gather_pieces(values0)

    reach = slots * share_rows
    tall = [((reach, block), BF16)] * 2
    wide = [((block, reach), BF16)] * 2
    rhs, _ = after((rhs, partner))
    upper, partner = call(
        turned_rhs, "turned_rhs", [(levels - 1, owned, half_columns, share_rows)] * 2, [rhs], 0
    )
    uppers = [upper, swap_core(partner)]
    low_tiles = prepare(split_tiles, "split_tiles", 0, factor_tiles, tiles_partner, [], tall, 2000)
    full = (sups, half_columns, block)
    scratch = [pltpu.VMEM(window, F32)]
    partial = call(
        functools.partial(update_lower, 0, 1), "update_middle", [full],
        [*places, *uppers, *low_tiles, *pieces0], 2, scratch,
    )[0]
    tiles, d_other, late = after((factor_tiles, d_other, partial))
    diags = [diag_inv, d_partner, d_other, swap_core(d_other)]
    low_turned = prepare(
        diag_by_tiles, "diag_by_tiles", 0, tiles, tiles_partner, diags, wide, 3000
    )
    late, low_turned = after((late, low_turned))
    middle, values1 = call(
        level_values, "level_values", [full, piece],
        [late, swap_cols(partial), diag_inv, d_partner], 0,
    )
    pieces1 = gather_pieces(values1)
    tiles, _ = after((factor_tiles, values1))
    top_tiles = prepare(split_tiles, "split_tiles", 1, tiles, tiles_partner, [], tall, 2000)
    base = call(
        functools.partial(update_lower, 1, 2), "update_top_low", [full],
        [*places, *uppers, *top_tiles, *pieces0], 2, scratch,
    )[0]

    partial = call(
        update_top, "update_top", [full], [*places, *top_tiles, base, *pieces1], 2, scratch
    )[0]
    tiles, _ = after((factor_tiles, partial))
    turned = prepare(
        gram_by_tiles, "gram_by_tiles", 1, tiles, tiles_partner, diags,
        wide + [((block, block), F32)], 3000,
    )
    top_turned, grams = turned[:2] + turned[3:5], [turned[2], turned[5]]
    residual, *out = call(
        top_carry, "top_carry", [full] + [piece] * PIECES,
        [*places, partial, swap_cols(partial), *top_turned], 2, scratch,
    )
    carried = sum(scatter_pieces(out))
    residual, _ = after((residual, carried))
    lowest, mine2, partner2, values1_other = call(
        lowest_carry, "lowest_carry", [window, shared, shared, piece],
        [*places, residual, *top_turned, *grams, middle, *diags[2:]], 2, cost=2000,
    )

    residual, *out = call(
        middle_carry, "middle_carry", [full] + [piece] * PIECES,
        [*places, carried, swap_cols(carried), values1, values1_other, *low_turned, lowest],
        2, scratch,
    )

    mine, partner = call(
        last_product, "last_product", [(owned, half_columns, block)] * 2,
        [values0, *scatter_pieces(out), diag_inv, d_partner], 0,
    )
    own, other = call(
        turned_solution, "turned_solution", [(owned, share_rows, columns)] * 2,
        [mine, swap_core(partner)], 0,
    )
    own = own + swap_cols(other)

    residual, partner2, _ = after((residual, partner2, other))
    mine1, partner1 = call(
        middle_solved, "middle_solved", [shared, shared], [residual, *diags], 0
    )
    result_upper = call(
        turned_upper, "turned_upper", [(levels - 1, owned, share_rows, columns)],
        [mine2, swap_core(partner2), mine1, swap_core(partner1)], 0,
    )[0]
    return jnp.concatenate([own[None], result_upper], 0)


def solution(mesh):
    placed = (
        P(None, "rows", "cols", None),
        P(None, "rows", "cols", None),
        P(None, "rows", None, "cols", None),
        P(None, "rows", None),
        P(None, "rows"),
    )
    small = mesh.shape["rows"] == 16 and mesh.shape["cols"] == 2
    return jax.shard_map(
        local if small else local_any,
        mesh=mesh,
        in_specs=placed,
        out_specs=P(None, "rows", "cols", None),
        check_vma=False,
    )
```

```python
import functools

import jax
import jax.numpy as jnp
from jax import lax
from jax.experimental import pallas as pl
from jax.experimental.pallas import tpu as pltpu
from jax.sharding import PartitionSpec as P

KDEV = 7


def from_behind(value, axis, steps):
    count = lax.axis_size(axis)
    leading, last = (max(0, -steps), min(count, count - steps))
    return lax.ppermute(value, axis, [(source, source + steps) for source in range(leading, last)])


def local_any(rhs, diag_inv, factor_tiles, tile_source, tile_count):
    levels = rhs.shape[0]
    owned_count = rhs.shape[1]
    share_rows = rhs.shape[2]
    columns = rhs.shape[3]
    slot_count = tile_source.shape[2]
    reach_dev = KDEV
    window_len = 2 * reach_dev + 1
    total_sup = lax.axis_size("rows") * owned_count
    row_place = lax.axis_index("rows")
    highest = lax.Precision.HIGHEST
    slot_ids = jnp.arange(slot_count, dtype=jnp.int32)

    def window_places(sources):
        src_level = sources // total_sup
        within = sources % total_sup
        return (
            src_level * window_len + within // owned_count - row_place + reach_dev
        ) * owned_count + within % owned_count

    def live_mask(counts):
        return (slot_ids[None, :] < counts[:, None]).astype(jnp.float32)

    def full_rows(piece):
        return lax.all_gather(piece, "cols", axis=1, tiled=True)

    forward_values = []
    windows = []
    for height in range(levels):
        if height == 0:
            whole_block = full_rows(rhs[0])
        else:
            stacked = jnp.stack(windows, 0).reshape(
                height * window_len * owned_count, share_rows, columns
            )
            places = window_places(tile_source[height - 1])
            picked = (
                jnp.take(stacked, places, axis=0)
                * live_mask(tile_count[height - 1])[:, :, None, None]
            )
            partial_value = jnp.einsum(
                "skci,skcr->sir", factor_tiles[height - 1], picked, precision=highest
            )
            whole_block = full_rows(
                rhs[height]
                - lax.psum_scatter(partial_value, "cols", scatter_dimension=1, tiled=True)
            )
        values = jnp.einsum("sci,sir->scr", diag_inv[height], whole_block, precision=highest)
        forward_values.append(values)
        if height + 1 < levels:
            pieces = []
            for pull_offset in range(-reach_dev, reach_dev + 1):
                if pull_offset == 0:
                    pieces.append(values)
                else:
                    pieces.append(from_behind(values, "rows", -pull_offset))
            windows.append(jnp.stack(pieces, 0))
    carried = [jnp.zeros_like(forward_values[0]) for height in range(levels)]
    solution = [None] * levels
    for height in reversed(range(levels)):
        partial_value = jnp.einsum(
            "sci,scr->sir",
            diag_inv[height],
            forward_values[height] - carried[height],
            precision=highest,
        )
        own_share = lax.psum_scatter(partial_value, "cols", scatter_dimension=1, tiled=True)
        if height > 0:
            whole_block = lax.all_gather(own_share, "cols", axis=1, tiled=True)
        solution[height] = own_share
        if height > 0:
            term_set = jnp.einsum(
                "skci,sir->skcr", factor_tiles[height - 1], whole_block, precision=highest
            )
            term_set = term_set * live_mask(tile_count[height - 1])[:, :, None, None]
            places = window_places(tile_source[height - 1]).reshape(-1)
            targets = height * window_len * owned_count
            one_hot = (jnp.arange(targets, dtype=jnp.int32)[:, None] == places[None, :]).astype(
                jnp.float32
            )
            outgoing = jnp.einsum(
                "ms,slg->mlg",
                one_hot,
                term_set.reshape(owned_count * slot_count, share_rows, columns),
                precision=highest,
            )
            push_outgoing = outgoing.reshape(height, window_len, owned_count, share_rows, columns)
            received = push_outgoing[:, reach_dev]
            for offset in range(-reach_dev, reach_dev + 1):
                if offset != 0:
                    received = received + from_behind(
                        push_outgoing[:, reach_dev + offset], "rows", offset
                    )
            for lower_level in range(height):
                carried[lower_level] = carried[lower_level] + received[lower_level]
    return jnp.stack(solution, 0)


F32 = jnp.float32
BF16 = jnp.bfloat16
NN = (((1,), (0,)), ((), ()))
NT = (((1,), (1,)), ((), ()))
PIECES = 8


def halves(value):
    high = value.astype(BF16)
    return high, (value - high.astype(F32)).astype(BF16)


def dot3(left, right, dims):
    left_high, left_low = halves(left)
    right_high, right_low = right if isinstance(right, tuple) else halves(right)
    dot = functools.partial(lax.dot_general, dimension_numbers=dims, preferred_element_type=F32)
    rows = left.shape[0]
    both = dot(jnp.concatenate([left_high, left_low], 0), right_high)
    return both[:rows] + both[rows:] + dot(left_high, right_low)


def ordered(mine, theirs, place, axis):
    first = jnp.where(place == 0, mine, theirs)
    second = jnp.where(place == 0, theirs, mine)
    return jnp.concatenate([first, second], axis)


VMEM_LIMIT = 20 * 1024 * 1024


def options(cost):
    return dict(
        cost_estimate=pl.CostEstimate(flops=cost * 1000000, bytes_accessed=0, transcendentals=0),
        compiler_params=pltpu.CompilerParams(vmem_limit_bytes=VMEM_LIMIT),
    )


def call(kernel, name, outs, args, scalars=1, scratch=(), cost=1000):
    in_specs = [pl.BlockSpec(memory_space=pltpu.SMEM)] * scalars
    in_specs += [pl.BlockSpec(memory_space=pltpu.VMEM)] * (len(args) - scalars)
    return pl.pallas_call(
        kernel,
        out_shape=[
            jax.ShapeDtypeStruct(*out) if isinstance(out[0], tuple) else jax.ShapeDtypeStruct(out, F32)
            for out in outs
        ],
        in_specs=in_specs,
        out_specs=[pl.BlockSpec(memory_space=pltpu.VMEM)] * len(outs),
        scratch_shapes=list(scratch),
        name=name,
        **options(cost),
    )(*args)


def put_halves(value, high_out, low_out, at):
    high, low = halves(value)
    high_out[at] = high
    low_out[at] = low


def split_kernel(own, partner, *outs):
    put_halves(own[0, 0].reshape(-1, own.shape[-1]), *outs[:2], 0)
    put_halves(partner[0, 0].reshape(-1, own.shape[-1]), *outs[2:], 0)


def split_tiles(level, own, partner):
    own = pltpu.with_memory_space_constraint(own, pltpu.HBM)
    owned, slots, depth, width = own.shape[1:]
    block_in = pl.BlockSpec((1, 1, slots, depth, width), lambda s: (level, s, 0, 0, 0))
    block_out = pl.BlockSpec((1, slots * depth, width), lambda s: (s, 0, 0))
    return pl.pallas_call(
        split_kernel,
        grid=(owned,),
        out_shape=[jax.ShapeDtypeStruct((owned, slots * depth, width), BF16)] * 4,
        in_specs=[block_in] * 2,
        out_specs=[block_out] * 4,
        name="split_tiles",
        **options(2000),
    )(own, partner)


def whole_diag(level, diags, s):
    own, partner, own_other, partner_other = diags
    half = own.shape[1]
    if s < half:
        pair = own[level, s], own_other[level - 1, s]
    else:
        pair = partner[level, s % half], partner_other[level - 1, s % half]
    return jnp.concatenate(pair, 0)


def diag_by_tiles(d0, d1, d2, d3, *refs):
    tiles, outs = refs[:4], refs[4:]
    half = d0.shape[1]
    for s in range(2 * half):
        value = dot3(whole_diag(1, (d0, d1, d2, d3), s), part_of(tiles, s), NT)
        put_halves(value, *(outs[:2] if s < half else outs[2:]), s % half)


def gram_by_tiles(d0, d1, d2, d3, *refs):
    tiles, grams, outs = refs[:4], refs[4], refs[5:]
    half = d0.shape[1]
    for s in range(2 * half):
        diag = whole_diag(2, (d0, d1, d2, d3), s)
        gram = dot3(diag.T, diag, NN)
        grams[s] = gram
        value = dot3(gram, part_of(tiles, s), NT)
        put_halves(value, *(outs[:2] if s < half else outs[2:]), s % half)


def part_of(parts, s):
    count = len(parts) // 2
    half = parts[0].shape[0]
    chosen = parts[:count] if s < half else parts[count:]
    return tuple(part[s % half] for part in chosen)


def first_values(rhs_own, rhs_other, diag, mine, partner):
    core, col = lax.axis_index("rows") % 2, lax.axis_index("cols")
    half = mine.shape[1]
    for s in range(rhs_own.shape[0]):
        rows = ordered(rhs_own[s], rhs_other[s], col, 0)
        values = dot3(diag[0, s], rows, NN).T
        low, high = values[:half], values[half:]
        mine[s] = jnp.where(core == 0, low, high)
        partner[s] = jnp.where(core == 0, high, low)


def first_call(rhs_own, rhs_other, diag):
    owned, depth, columns = rhs_own.shape
    whole = pl.BlockSpec((owned, depth, columns), lambda i: (0, 0, 0))
    half = pl.BlockSpec((owned, columns // 2, depth), lambda i: (0, 0, 0))
    return pl.pallas_call(
        first_values,
        grid=(1,),
        out_shape=[jax.ShapeDtypeStruct((owned, columns // 2, depth), F32)] * 2,
        in_specs=[
            whole, whole,
            pl.BlockSpec((1,) + diag.shape[1:], lambda i: (0, 0, 0, 0)),
        ],
        out_specs=[half, half],
        name="first_values",
        **options(500),
    )(rhs_own, rhs_other, pltpu.with_memory_space_constraint(diag, pltpu.HBM))


def slot_places(sources, counts, places):
    row = lax.axis_index("rows")
    levels, owned, slots = sources.shape
    total = lax.axis_size("rows") * owned
    for l in range(levels):
        for s in range(owned):
            for k in range(slots):
                source = sources[l, s, k]
                live = k < counts[l, s]
                lower = jnp.where(source >= total, 1, 0)
                within = source - lower * total
                place = (row ^ (within // owned)) * owned + within % owned
                at = s * slots + k
                if l == 0:
                    places[0, at] = jnp.where(live, place, -1)
                else:
                    places[1, at] = jnp.where(live & (lower == 0), place, -1)
                    places[2, at] = jnp.where(live & (lower == 1), place, -1)


def place_of(places, index, slot, owned):
    own, partner = places
    count = own.shape[1]
    if slot < count:
        place = own[index, slot]
        return jnp.maximum(place, 0), place >= 0
    place = partner[index, slot - count]
    return jnp.where(place >= 0, place ^ owned, 0), place >= 0


def turned_rhs(rhs, mine, partner):
    core = lax.axis_index("rows") % 2
    half = mine.shape[2]
    for l in range(mine.shape[0]):
        for s in range(mine.shape[1]):
            rows = rhs[l + 1, s].T
            low, high = rows[:half], rows[half:]
            mine[l, s] = jnp.where(core == 0, low, high)
            partner[l, s] = jnp.where(core == 0, high, low)


def gathered(index, places, pieces, window):
    sups = pieces[0].shape[0]
    slots = 2 * places[0].shape[1] // sups
    for number, piece in enumerate(pieces):
        window[number * sups : (number + 1) * sups] = piece[...]
    for s in range(sups):
        picked = []
        for k in range(slots):
            place, live = place_of(places, index, s * slots + k, sups // 2)
            picked.append(jnp.where(live, window[place], 0.0))
        yield jnp.concatenate(picked, 1)


def upper_of(level, mine, partner, s):
    half = mine.shape[1]
    return mine[level - 1, s] if s < half else partner[level - 1, s % half]


def lower_residuals(index, level, places, rhs, tiles, pieces, window):
    col = lax.axis_index("cols")
    for s, left in enumerate(gathered(index, places, pieces, window)):
        right = upper_of(level, *rhs, s)
        zero = jnp.zeros_like(right)
        base = jnp.concatenate([jnp.where(col == 0, right, zero), jnp.where(col == 0, zero, right)], 1)
        yield base - dot3(left, part_of(tiles, s), NN)


def update_middle(places, places_partner, rhs, rhs_partner, *refs):
    tiles, diags, pieces, (own, other, window) = refs[:4], refs[4:8], refs[8:-3], refs[-3:]
    depth = own.shape[2]
    residuals = lower_residuals(
        0, 1, (places, places_partner), (rhs, rhs_partner), tiles, pieces, window
    )
    for s, residual in enumerate(residuals):
        values = dot3(residual, whole_diag(1, diags, s), NT)
        own[s] = values[:, :depth]
        other[s] = values[:, depth:]


def update_top_low(places, places_partner, rhs, rhs_partner, *refs):
    tiles, pieces, (out, window) = refs[:4], refs[4:-2], refs[-2:]
    residuals = lower_residuals(
        1, 2, (places, places_partner), (rhs, rhs_partner), tiles, pieces, window
    )
    for s, residual in enumerate(residuals):
        out[s] = residual


def update_top(places, places_partner, *refs):
    tiles, base, pieces, (out, window) = refs[:4], refs[4], refs[5:-2], refs[-2:]
    for s, left in enumerate(gathered(2, (places, places_partner), pieces, window)):
        out[s] = base[s] - dot3(left, part_of(tiles, s), NN)


def add_terms(index, places, tiles, left, s, totals):
    owned = tiles[0].shape[0]
    depth = totals.shape[2]
    terms = dot3(left, part_of(tiles, s), NN)
    slots = terms.shape[1] // depth
    for k in range(slots):
        place, live = place_of(places, index, s * slots + k, owned)
        term = jnp.where(live, terms[:, k * depth : (k + 1) * depth], 0.0)
        totals[place] = totals[place] + term


def share_out(col, x, s, solved_mine, solved_partner):
    depth = solved_mine.shape[2]
    half = solved_mine.shape[0]
    share = jnp.where(col == 0, x[:, :depth], x[:, depth:])
    if s < half:
        solved_mine[s] = share
    else:
        solved_partner[s % half] = share


def pieces_out(totals, outs):
    first = 0
    for out in outs:
        out[...] = totals[first : first + out.shape[0]]
        first += out.shape[0]


def top_carry(places, places_partner, mine, theirs, t0, t1, t2, t3, residual, *rest):
    outs, totals = rest[:-1], rest[-1]
    totals[...] = jnp.zeros_like(totals)
    for s in range(residual.shape[0]):
        left = mine[s] + theirs[s]
        residual[s] = left
        add_terms(2, (places, places_partner), (t0, t1, t2, t3), left, s, totals)
    pieces_out(totals, outs)


def lowest_carry(
    places, places_partner, residual, t0, t1, t2, t3, grams,
    totals, solved_mine, solved_partner,
):
    totals[...] = jnp.zeros_like(totals)
    col = lax.axis_index("cols")
    for s in range(residual.shape[0]):
        share_out(col, dot3(residual[s], grams[s], NN), s, solved_mine, solved_partner)
        add_terms(1, (places, places_partner), (t0, t1, t2, t3), residual[s], s, totals)


def middle_carry(
    places, places_partner, own, other, d0, d1, d2, d3, t0, t1, t2, t3,
    lowest, solved_mine, solved_partner, *rest
):
    outs, totals = rest[:-1], rest[-1]
    totals[...] = lowest[...]
    for s in range(own.shape[0]):
        left = jnp.concatenate([own[s], other[s]], 1)
        add_terms(0, (places, places_partner), (t0, t1, t2, t3), left, s, totals)
        x = dot3(left, whole_diag(1, (d0, d1, d2, d3), s), NN)
        share_out(lax.axis_index("cols"), x, s, solved_mine, solved_partner)
    pieces_out(totals, outs)


def last_product(values, a, b, c, d, e, d_own, d_partner, mine, partner):
    sups = values.shape[0]
    half = sups // 2
    for s in range(sups):
        carried = a[s] + b[s] + c[s] + d[s] + e[s]
        diag, out = (d_own, mine) if s < half else (d_partner, partner)
        out[s % half] = dot3(values[s] - carried, diag[0, s % half], NN)


def turned_solution(mine, partner, own, other):
    core, col = lax.axis_index("rows") % 2, lax.axis_index("cols")
    depth = own.shape[1]
    for s in range(mine.shape[0]):
        both = ordered(mine[s], partner[s], core, 0)
        low, high = both[:, :depth].T, both[:, depth:].T
        own[s] = jnp.where(col == 0, low, high)
        other[s] = jnp.where(col == 0, high, low)


def turned_upper(mine2, partner2, mine1, partner1, out):
    core = lax.axis_index("rows") % 2
    for s in range(mine2.shape[0]):
        out[0, s] = ordered(mine1[s], partner1[s], core, 0).T
        out[1, s] = ordered(mine2[s], partner2[s], core, 0).T


def local(rhs, diag_inv, factor_tiles, tile_source, tile_count):
    levels, owned, share_rows, columns = rhs.shape
    slots = tile_source.shape[2]
    sups = 2 * owned
    block = share_rows * 2
    half_columns = columns // 2
    rows_total = lax.axis_size("rows")
    piece = (sups, half_columns, share_rows)
    shared = (owned, half_columns, share_rows)
    window = (PIECES * sups, half_columns, share_rows)
    after = lax.optimization_barrier

    def swap_cols(value):
        return lax.ppermute(value, "cols", [(0, 1), (1, 0)])

    def swap_rows(value, bits):
        return lax.ppermute(value, "rows", [(r, r ^ bits) for r in range(rows_total)])

    def swap_core(value):
        return swap_rows(value, 1)

    def swap_x(value):
        return swap_rows(value, 2)

    def swap_mid(value):
        low, high = rows_total // 4, 3 * rows_total // 4
        pairs = [(r, r ^ 12 if low <= r < high else r ^ 2) for r in range(rows_total)]
        return lax.ppermute(value, "rows", pairs)

    def gather_pieces(value):
        far = swap_rows(value, 8)
        beside = swap_x(value)
        mid = swap_mid(value)
        near = swap_rows(value, 4)
        return [
            value, beside, near, swap_rows(beside, 4), far, swap_x(far), mid, swap_mid(beside)
        ]

    def scatter_pieces(p):
        far = swap_rows(p[4] + swap_x(p[5]), 8)
        mid = swap_mid(p[6] + swap_x(p[7]))
        beside = swap_x(p[1] + swap_rows(p[3], 4))
        near = swap_rows(p[2], 4)
        return [p[0], near, far, mid, beside]

    rhs0 = rhs[0]
    rhs0_other = swap_cols(rhs0)
    d_partner = swap_core(diag_inv)
    tiles_partner = swap_core(factor_tiles)
    own_places = pl.pallas_call(
        slot_places,
        out_shape=jax.ShapeDtypeStruct((levels, owned * slots), jnp.int32),
        in_specs=[pl.BlockSpec(memory_space=pltpu.SMEM)] * 2,
        out_specs=pl.BlockSpec(memory_space=pltpu.SMEM),
        name="slot_places",
        **options(500),
    )(tile_source, tile_count)
    places = [own_places, swap_core(own_places)]
    diag, rhs0 = after((diag_inv, rhs0))
    d_other = swap_cols(diag[1:])
    rhs0, places, tiles_partner, d_partner = after((rhs0, places, tiles_partner, d_partner))
    mine, partner = first_call(rhs0, rhs0_other, diag_inv)
    values0 = jnp.concatenate([mine, swap_core(partner)], 0)
    pieces0 = gather_pieces(values0)

    reach = slots * share_rows
    wide = [((owned, block, reach), BF16)] * 4
    rhs, _ = after((rhs, partner))
    upper, partner = call(
        turned_rhs, "turned_rhs", [(levels - 1, owned, half_columns, share_rows)] * 2, [rhs], 0
    )
    uppers = [upper, swap_core(partner)]
    low_tiles = split_tiles(0, factor_tiles, tiles_partner)
    full = (sups, half_columns, block)
    scratch = [pltpu.VMEM(window, F32)]
    d_other, _ = after((d_other, (low_tiles, uppers, pieces0)))
    diags = [diag_inv, d_partner, d_other, swap_core(d_other)]
    own, other = call(
        update_middle, "update_middle", [piece] * 2,
        [*places, *uppers, *low_tiles, *diags, *pieces0], 2, scratch,
    )
    values1 = own + swap_cols(other)
    pieces1 = gather_pieces(values1)
    tiles, _ = after((factor_tiles, values1))
    top_tiles = split_tiles(1, tiles, tiles_partner)
    base = call(
        update_top_low, "update_top_low", [full],
        [*places, *uppers, *top_tiles, *pieces0], 2, scratch,
    )[0]

    partial = call(
        update_top, "update_top", [full], [*places, *top_tiles, base, *pieces1], 2, scratch
    )[0]
    top_ready, _ = after((top_tiles, partial))
    grams, *top_turned = call(
        gram_by_tiles, "gram_by_tiles", [(sups, block, block)] + wide, [*diags, *top_ready], 0,
        cost=3000,
    )
    residual, *out = call(
        top_carry, "top_carry", [full] + [piece] * PIECES,
        [*places, partial, swap_cols(partial), *top_turned], 2, scratch,
    )
    carried = values1 - functools.reduce(jnp.add, scatter_pieces(out))
    residual, low_ready, _ = after((residual, low_tiles, carried))
    low_turned = call(diag_by_tiles, "diag_by_tiles", wide, [*diags, *low_ready], 0, cost=3000)
    lowest, mine2, partner2 = call(
        lowest_carry, "lowest_carry", [window, shared, shared],
        [*places, residual, *top_turned, grams], 2, cost=2000,
    )

    mine1, partner1, *out = call(
        middle_carry, "middle_carry", [shared, shared] + [piece] * PIECES,
        [*places, carried, swap_cols(carried), *diags, *low_turned, lowest],
        2, scratch,
    )

    mine, partner = call(
        last_product, "last_product", [(owned, half_columns, block)] * 2,
        [values0, *scatter_pieces(out), diag_inv, d_partner], 0,
    )
    own, other = call(
        turned_solution, "turned_solution", [(owned, share_rows, columns)] * 2,
        [mine, swap_core(partner)], 0,
    )
    own = own + swap_cols(other)

    partner1, partner2, _ = after((partner1, partner2, mine))
    result_upper = call(
        turned_upper, "turned_upper", [(levels - 1, owned, share_rows, columns)],
        [mine2, swap_core(partner2), mine1, swap_core(partner1)], 0,
    )[0]
    return jnp.concatenate([own[None], result_upper], 0)


def solution(mesh):
    placed = (
        P(None, "rows", "cols", None),
        P(None, "rows", "cols", None),
        P(None, "rows", None, "cols", None),
        P(None, "rows", None),
        P(None, "rows"),
    )
    small = mesh.shape["rows"] == 16 and mesh.shape["cols"] == 2
    return jax.shard_map(
        local if small else local_any,
        mesh=mesh,
        in_specs=placed,
        out_specs=P(None, "rows", "cols", None),
        check_vma=False,
    )
```

```python
import functools

import jax
import jax.numpy as jnp
from jax import lax
from jax.experimental import pallas as pl
from jax.experimental.pallas import tpu as pltpu
from jax.sharding import PartitionSpec as P

KDEV = 7


def from_behind(value, axis, steps):
    count = lax.axis_size(axis)
    leading, last = (max(0, -steps), min(count, count - steps))
    return lax.ppermute(value, axis, [(source, source + steps) for source in range(leading, last)])


def local_any(rhs, diag_inv, factor_tiles, tile_source, tile_count):
    levels = rhs.shape[0]
    owned_count = rhs.shape[1]
    share_rows = rhs.shape[2]
    columns = rhs.shape[3]
    slot_count = tile_source.shape[2]
    reach_dev = KDEV
    window_len = 2 * reach_dev + 1
    total_sup = lax.axis_size("rows") * owned_count
    row_place = lax.axis_index("rows")
    highest = lax.Precision.HIGHEST
    slot_ids = jnp.arange(slot_count, dtype=jnp.int32)

    def window_places(sources):
        src_level = sources // total_sup
        within = sources % total_sup
        return (
            src_level * window_len + within // owned_count - row_place + reach_dev
        ) * owned_count + within % owned_count

    def live_mask(counts):
        return (slot_ids[None, :] < counts[:, None]).astype(jnp.float32)

    def full_rows(piece):
        return lax.all_gather(piece, "cols", axis=1, tiled=True)

    forward_values = []
    windows = []
    for height in range(levels):
        if height == 0:
            whole_block = full_rows(rhs[0])
        else:
            stacked = jnp.stack(windows, 0).reshape(
                height * window_len * owned_count, share_rows, columns
            )
            places = window_places(tile_source[height - 1])
            picked = (
                jnp.take(stacked, places, axis=0)
                * live_mask(tile_count[height - 1])[:, :, None, None]
            )
            partial_value = jnp.einsum(
                "skci,skcr->sir", factor_tiles[height - 1], picked, precision=highest
            )
            whole_block = full_rows(
                rhs[height]
                - lax.psum_scatter(partial_value, "cols", scatter_dimension=1, tiled=True)
            )
        values = jnp.einsum("sci,sir->scr", diag_inv[height], whole_block, precision=highest)
        forward_values.append(values)
        if height + 1 < levels:
            pieces = []
            for pull_offset in range(-reach_dev, reach_dev + 1):
                if pull_offset == 0:
                    pieces.append(values)
                else:
                    pieces.append(from_behind(values, "rows", -pull_offset))
            windows.append(jnp.stack(pieces, 0))
    carried = [jnp.zeros_like(forward_values[0]) for height in range(levels)]
    solution = [None] * levels
    for height in reversed(range(levels)):
        partial_value = jnp.einsum(
            "sci,scr->sir",
            diag_inv[height],
            forward_values[height] - carried[height],
            precision=highest,
        )
        own_share = lax.psum_scatter(partial_value, "cols", scatter_dimension=1, tiled=True)
        if height > 0:
            whole_block = lax.all_gather(own_share, "cols", axis=1, tiled=True)
        solution[height] = own_share
        if height > 0:
            term_set = jnp.einsum(
                "skci,sir->skcr", factor_tiles[height - 1], whole_block, precision=highest
            )
            term_set = term_set * live_mask(tile_count[height - 1])[:, :, None, None]
            places = window_places(tile_source[height - 1]).reshape(-1)
            targets = height * window_len * owned_count
            one_hot = (jnp.arange(targets, dtype=jnp.int32)[:, None] == places[None, :]).astype(
                jnp.float32
            )
            outgoing = jnp.einsum(
                "ms,slg->mlg",
                one_hot,
                term_set.reshape(owned_count * slot_count, share_rows, columns),
                precision=highest,
            )
            push_outgoing = outgoing.reshape(height, window_len, owned_count, share_rows, columns)
            received = push_outgoing[:, reach_dev]
            for offset in range(-reach_dev, reach_dev + 1):
                if offset != 0:
                    received = received + from_behind(
                        push_outgoing[:, reach_dev + offset], "rows", offset
                    )
            for lower_level in range(height):
                carried[lower_level] = carried[lower_level] + received[lower_level]
    return jnp.stack(solution, 0)


F32 = jnp.float32
BF16 = jnp.bfloat16
NN = (((1,), (0,)), ((), ()))
NT = (((1,), (1,)), ((), ()))
PIECES = 8


def halves(value):
    high = value.astype(BF16)
    return high, (value - high.astype(F32)).astype(BF16)


def dot3(left, right, dims):
    left_high, left_low = halves(left)
    right_high, right_low = right if isinstance(right, tuple) else halves(right)
    dot = functools.partial(lax.dot_general, dimension_numbers=dims, preferred_element_type=F32)
    rows = left.shape[0]
    both = dot(jnp.concatenate([left_high, left_low], 0), right_high)
    return both[:rows] + both[rows:] + dot(left_high, right_low)


def ordered(mine, theirs, place, axis):
    first = jnp.where(place == 0, mine, theirs)
    second = jnp.where(place == 0, theirs, mine)
    return jnp.concatenate([first, second], axis)


VMEM_LIMIT = 20 * 1024 * 1024


def options(cost):
    return dict(
        cost_estimate=pl.CostEstimate(flops=cost * 1000000, bytes_accessed=0, transcendentals=0),
        compiler_params=pltpu.CompilerParams(vmem_limit_bytes=VMEM_LIMIT),
    )


def call(kernel, name, outs, args, scalars=1, scratch=(), cost=1000):
    in_specs = [pl.BlockSpec(memory_space=pltpu.SMEM)] * scalars
    in_specs += [pl.BlockSpec(memory_space=pltpu.VMEM)] * (len(args) - scalars)
    return pl.pallas_call(
        kernel,
        out_shape=[
            jax.ShapeDtypeStruct(*out) if isinstance(out[0], tuple) else jax.ShapeDtypeStruct(out, F32)
            for out in outs
        ],
        in_specs=in_specs,
        out_specs=[pl.BlockSpec(memory_space=pltpu.VMEM)] * len(outs),
        scratch_shapes=list(scratch),
        name=name,
        **options(cost),
    )(*args)


def put_halves(value, high_out, low_out, at):
    high, low = halves(value)
    high_out[at] = high
    low_out[at] = low


def split_kernel(own, partner, *outs):
    put_halves(own[0, 0].reshape(-1, own.shape[-1]), *outs[:2], 0)
    put_halves(partner[0, 0].reshape(-1, own.shape[-1]), *outs[2:], 0)


def split_tiles(level, own, partner):
    own = pltpu.with_memory_space_constraint(own, pltpu.HBM)
    owned, slots, depth, width = own.shape[1:]
    block_in = pl.BlockSpec((1, 1, slots, depth, width), lambda s: (level, s, 0, 0, 0))
    block_out = pl.BlockSpec((1, slots * depth, width), lambda s: (s, 0, 0))
    return pl.pallas_call(
        split_kernel,
        grid=(owned,),
        out_shape=[jax.ShapeDtypeStruct((owned, slots * depth, width), BF16)] * 4,
        in_specs=[block_in] * 2,
        out_specs=[block_out] * 4,
        name="split_tiles",
        **options(2000),
    )(own, partner)


def whole_diag(level, diags, s):
    own, partner, own_other, partner_other = diags
    half = own.shape[1]
    if s < half:
        pair = own[level, s], own_other[level - 1, s]
    else:
        pair = partner[level, s % half], partner_other[level - 1, s % half]
    return jnp.concatenate(pair, 0)


def diag_by_tiles(d0, d1, d2, d3, *refs):
    tiles, outs = refs[:4], refs[4:]
    half = d0.shape[1]
    for s in range(2 * half):
        value = dot3(whole_diag(1, (d0, d1, d2, d3), s), part_of(tiles, s), NT)
        put_halves(value, *(outs[:2] if s < half else outs[2:]), s % half)


def gram_by_tiles(d0, d1, d2, d3, *refs):
    tiles, grams, outs = refs[:4], refs[4], refs[5:]
    half = d0.shape[1]
    for s in range(2 * half):
        diag = whole_diag(2, (d0, d1, d2, d3), s)
        gram = dot3(diag.T, diag, NN)
        grams[s] = gram
        value = dot3(gram, part_of(tiles, s), NT)
        put_halves(value, *(outs[:2] if s < half else outs[2:]), s % half)


def part_of(parts, s):
    count = len(parts) // 2
    half = parts[0].shape[0]
    chosen = parts[:count] if s < half else parts[count:]
    return tuple(part[s % half] for part in chosen)


def first_values(rhs_own, rhs_other, diag, mine, partner):
    core, col = lax.axis_index("rows") % 2, lax.axis_index("cols")
    half = mine.shape[1]
    for s in range(rhs_own.shape[0]):
        rows = ordered(rhs_own[s], rhs_other[s], col, 0)
        values = dot3(diag[0, s], rows, NN).T
        low, high = values[:half], values[half:]
        mine[s] = jnp.where(core == 0, low, high)
        partner[s] = jnp.where(core == 0, high, low)


def first_call(rhs_own, rhs_other, diag):
    owned, depth, columns = rhs_own.shape
    whole = pl.BlockSpec((owned, depth, columns), lambda i: (0, 0, 0))
    half = pl.BlockSpec((owned, columns // 2, depth), lambda i: (0, 0, 0))
    return pl.pallas_call(
        first_values,
        grid=(1,),
        out_shape=[jax.ShapeDtypeStruct((owned, columns // 2, depth), F32)] * 2,
        in_specs=[
            whole, whole,
            pl.BlockSpec((1,) + diag.shape[1:], lambda i: (0, 0, 0, 0)),
        ],
        out_specs=[half, half],
        name="first_values",
        **options(500),
    )(rhs_own, rhs_other, pltpu.with_memory_space_constraint(diag, pltpu.HBM))


def slot_places(sources, counts, places):
    row = lax.axis_index("rows")
    levels, owned, slots = sources.shape
    total = lax.axis_size("rows") * owned
    for l in range(levels):
        for s in range(owned):
            for k in range(slots):
                source = sources[l, s, k]
                live = k < counts[l, s]
                lower = jnp.where(source >= total, 1, 0)
                within = source - lower * total
                place = (row ^ (within // owned)) * owned + within % owned
                at = s * slots + k
                if l == 0:
                    places[0, at] = jnp.where(live, place, -1)
                else:
                    places[1, at] = jnp.where(live & (lower == 0), place, -1)
                    places[2, at] = jnp.where(live & (lower == 1), place, -1)


def place_of(places, index, slot, owned):
    own, partner = places
    count = own.shape[1]
    if slot < count:
        place = own[index, slot]
        return jnp.maximum(place, 0), place >= 0
    place = partner[index, slot - count]
    return jnp.where(place >= 0, place ^ owned, 0), place >= 0


def turned_rhs(rhs, mine, partner):
    core = lax.axis_index("rows") % 2
    half = mine.shape[2]
    for l in range(mine.shape[0]):
        for s in range(mine.shape[1]):
            rows = rhs[l + 1, s].T
            low, high = rows[:half], rows[half:]
            mine[l, s] = jnp.where(core == 0, low, high)
            partner[l, s] = jnp.where(core == 0, high, low)


def gathered(index, places, pieces, window):
    sups = pieces[0].shape[0]
    slots = 2 * places[0].shape[1] // sups
    for number, piece in enumerate(pieces):
        window[number * sups : (number + 1) * sups] = piece[...]
    for s in range(sups):
        picked = []
        for k in range(slots):
            place, live = place_of(places, index, s * slots + k, sups // 2)
            picked.append(jnp.where(live, window[place], 0.0))
        yield jnp.concatenate(picked, 1)


def upper_of(level, mine, partner, s):
    half = mine.shape[1]
    return mine[level - 1, s] if s < half else partner[level - 1, s % half]


def update_lower(index, level, places, places_partner, rhs, rhs_partner, *refs):
    tiles, pieces, (out, window) = refs[:4], refs[4:-2], refs[-2:]
    col = lax.axis_index("cols")
    for s, left in enumerate(gathered(index, (places, places_partner), pieces, window)):
        right = upper_of(level, rhs, rhs_partner, s)
        zero = jnp.zeros_like(right)
        base = jnp.concatenate([jnp.where(col == 0, right, zero), jnp.where(col == 0, zero, right)], 1)
        out[s] = base - dot3(left, part_of(tiles, s), NN)


def middle_values(residual, d0, d1, d2, d3, own, other):
    depth = own.shape[2]
    for s in range(own.shape[0]):
        values = dot3(residual[s], whole_diag(1, (d0, d1, d2, d3), s), NT)
        own[s] = values[:, :depth]
        other[s] = values[:, depth:]


def update_top(places, places_partner, *refs):
    tiles, base, pieces, (out, window) = refs[:4], refs[4], refs[5:-2], refs[-2:]
    for s, left in enumerate(gathered(2, (places, places_partner), pieces, window)):
        out[s] = base[s] - dot3(left, part_of(tiles, s), NN)


def add_terms(index, places, tiles, left, s, totals):
    owned = tiles[0].shape[0]
    depth = totals.shape[2]
    terms = dot3(left, part_of(tiles, s), NN)
    slots = terms.shape[1] // depth
    for k in range(slots):
        place, live = place_of(places, index, s * slots + k, owned)
        term = jnp.where(live, terms[:, k * depth : (k + 1) * depth], 0.0)
        totals[place] = totals[place] + term


def share_out(col, x, s, solved_mine, solved_partner):
    depth = solved_mine.shape[2]
    half = solved_mine.shape[0]
    share = jnp.where(col == 0, x[:, :depth], x[:, depth:])
    if s < half:
        solved_mine[s] = share
    else:
        solved_partner[s % half] = share


def pieces_out(totals, outs):
    first = 0
    for out in outs:
        out[...] = totals[first : first + out.shape[0]]
        first += out.shape[0]


def top_carry(places, places_partner, mine, theirs, t0, t1, t2, t3, residual, *rest):
    outs, totals = rest[:-1], rest[-1]
    totals[...] = jnp.zeros_like(totals)
    for s in range(residual.shape[0]):
        left = mine[s] + theirs[s]
        residual[s] = left
        add_terms(2, (places, places_partner), (t0, t1, t2, t3), left, s, totals)
    pieces_out(totals, outs)


def lowest_carry(
    places, places_partner, residual, t0, t1, t2, t3, grams,
    totals, solved_mine, solved_partner,
):
    totals[...] = jnp.zeros_like(totals)
    col = lax.axis_index("cols")
    for s in range(residual.shape[0]):
        share_out(col, dot3(residual[s], grams[s], NN), s, solved_mine, solved_partner)
        add_terms(1, (places, places_partner), (t0, t1, t2, t3), residual[s], s, totals)


def middle_carry(
    places, places_partner, own, other, d0, d1, d2, d3, t0, t1, t2, t3,
    lowest, solved_mine, solved_partner, *rest
):
    outs, totals = rest[:-1], rest[-1]
    totals[...] = lowest[...]
    for s in range(own.shape[0]):
        left = jnp.concatenate([own[s], other[s]], 1)
        add_terms(0, (places, places_partner), (t0, t1, t2, t3), left, s, totals)
        x = dot3(left, whole_diag(1, (d0, d1, d2, d3), s), NN)
        share_out(lax.axis_index("cols"), x, s, solved_mine, solved_partner)
    pieces_out(totals, outs)


def last_product(values, a, b, c, d, e, d_own, d_partner, mine, partner):
    sups = values.shape[0]
    half = sups // 2
    for s in range(sups):
        carried = a[s] + b[s] + c[s] + d[s] + e[s]
        diag, out = (d_own, mine) if s < half else (d_partner, partner)
        out[s % half] = dot3(values[s] - carried, diag[0, s % half], NN)


def turned_solution(mine, partner, own, other):
    core, col = lax.axis_index("rows") % 2, lax.axis_index("cols")
    depth = own.shape[1]
    for s in range(mine.shape[0]):
        both = ordered(mine[s], partner[s], core, 0)
        low, high = both[:, :depth].T, both[:, depth:].T
        own[s] = jnp.where(col == 0, low, high)
        other[s] = jnp.where(col == 0, high, low)


def turned_upper(mine2, partner2, mine1, partner1, out):
    core = lax.axis_index("rows") % 2
    for s in range(mine2.shape[0]):
        out[0, s] = ordered(mine1[s], partner1[s], core, 0).T
        out[1, s] = ordered(mine2[s], partner2[s], core, 0).T


def local(rhs, diag_inv, factor_tiles, tile_source, tile_count):
    levels, owned, share_rows, columns = rhs.shape
    slots = tile_source.shape[2]
    sups = 2 * owned
    block = share_rows * 2
    half_columns = columns // 2
    rows_total = lax.axis_size("rows")
    piece = (sups, half_columns, share_rows)
    shared = (owned, half_columns, share_rows)
    window = (PIECES * sups, half_columns, share_rows)
    after = lax.optimization_barrier

    def swap_cols(value):
        return lax.ppermute(value, "cols", [(0, 1), (1, 0)])

    def swap_rows(value, bits):
        return lax.ppermute(value, "rows", [(r, r ^ bits) for r in range(rows_total)])

    def swap_core(value):
        return swap_rows(value, 1)

    def swap_x(value):
        return swap_rows(value, 2)

    def swap_mid(value):
        low, high = rows_total // 4, 3 * rows_total // 4
        pairs = [(r, r ^ 12 if low <= r < high else r ^ 2) for r in range(rows_total)]
        return lax.ppermute(value, "rows", pairs)

    def gather_pieces(value):
        far = swap_rows(value, 8)
        beside = swap_x(value)
        mid = swap_mid(value)
        near = swap_rows(value, 4)
        return [
            value, beside, near, swap_rows(beside, 4), far, swap_x(far), mid, swap_mid(beside)
        ]

    def scatter_upper(p):
        far = swap_rows(p[4] + swap_x(p[5]), 8)
        beside = swap_x(p[1] + (swap_mid(p[7]) + swap_rows(p[3], 4)))
        mid = swap_mid(p[6])
        near = swap_rows(p[2], 4)
        return [p[0], far, beside, mid, near]

    def scatter_lowest(p):
        far = swap_rows(p[4] + swap_x(p[5]), 8)
        beside = swap_x(p[1] + (swap_mid(p[7]) + swap_rows(p[3], 4)))
        mid = swap_mid(p[6])
        near = swap_rows(p[2], 4)
        return [p[0], near, mid, beside, far]

    rhs0 = rhs[0]
    rhs0_other = swap_cols(rhs0)
    d_partner = swap_core(diag_inv)
    tiles_partner = swap_core(factor_tiles)
    own_places = pl.pallas_call(
        slot_places,
        out_shape=jax.ShapeDtypeStruct((levels, owned * slots), jnp.int32),
        in_specs=[pl.BlockSpec(memory_space=pltpu.SMEM)] * 2,
        out_specs=pl.BlockSpec(memory_space=pltpu.SMEM),
        name="slot_places",
        **options(500),
    )(tile_source, tile_count)
    places = [own_places, swap_core(own_places)]
    diag, rhs0 = after((diag_inv, rhs0))
    d_other = swap_cols(diag[1:])
    rhs0, places, tiles_partner, d_partner = after((rhs0, places, tiles_partner, d_partner))
    mine, partner = first_call(rhs0, rhs0_other, diag_inv)
    values0 = jnp.concatenate([mine, swap_core(partner)], 0)
    pieces0 = gather_pieces(values0)

    reach = slots * share_rows
    wide = [((owned, block, reach), BF16)] * 4
    rhs, _ = after((rhs, partner))
    upper, partner = call(
        turned_rhs, "turned_rhs", [(levels - 1, owned, half_columns, share_rows)] * 2, [rhs], 0
    )
    uppers = [upper, swap_core(partner)]
    low_tiles = split_tiles(0, factor_tiles, tiles_partner)
    full = (sups, half_columns, block)
    scratch = [pltpu.VMEM(window, F32)]
    d_other, _ = after((d_other, (low_tiles, uppers, pieces0)))
    diags = [diag_inv, d_partner, d_other, swap_core(d_other)]
    partial = call(
        functools.partial(update_lower, 0, 1), "update_middle", [full],
        [*places, *uppers, *low_tiles, *pieces0], 2, scratch,
    )[0]
    own, other = call(middle_values, "middle_values", [piece] * 2, [partial, *diags], 0)
    values1 = own + swap_cols(other)
    pieces1 = gather_pieces(values1)
    tiles, _ = after((factor_tiles, values1))
    top_tiles = split_tiles(1, tiles, tiles_partner)
    base = call(
        functools.partial(update_lower, 1, 2), "update_top_low", [full],
        [*places, *uppers, *top_tiles, *pieces0], 2, scratch,
    )[0]

    partial = call(
        update_top, "update_top", [full], [*places, *top_tiles, base, *pieces1], 2, scratch
    )[0]
    top_ready, _ = after((top_tiles, partial))
    grams, *top_turned = call(
        gram_by_tiles, "gram_by_tiles", [(sups, block, block)] + wide, [*diags, *top_ready], 0,
        cost=3000,
    )
    residual, *out = call(
        top_carry, "top_carry", [full] + [piece] * PIECES,
        [*places, partial, swap_cols(partial), *top_turned], 2, scratch,
    )
    carried = values1 - functools.reduce(jnp.add, scatter_upper(out))
    residual, low_ready, _ = after((residual, low_tiles, carried))
    low_turned = call(diag_by_tiles, "diag_by_tiles", wide, [*diags, *low_ready], 0, cost=3000)
    lowest, mine2, partner2 = call(
        lowest_carry, "lowest_carry", [window, shared, shared],
        [*places, residual, *top_turned, grams], 2, cost=2000,
    )

    mine1, partner1, *out = call(
        middle_carry, "middle_carry", [shared, shared] + [piece] * PIECES,
        [*places, carried, swap_cols(carried), *diags, *low_turned, lowest],
        2, scratch,
    )

    mine, partner = call(
        last_product, "last_product", [(owned, half_columns, block)] * 2,
        [values0, *scatter_lowest(out), diag_inv, d_partner], 0,
    )
    own, other = call(
        turned_solution, "turned_solution", [(owned, share_rows, columns)] * 2,
        [mine, swap_core(partner)], 0,
    )
    own = own + swap_cols(other)

    partner1, partner2, _ = after((partner1, partner2, mine))
    result_upper = call(
        turned_upper, "turned_upper", [(levels - 1, owned, share_rows, columns)],
        [mine2, swap_core(partner2), mine1, swap_core(partner1)], 0,
    )[0]
    return jnp.concatenate([own[None], result_upper], 0)


def solution(mesh):
    placed = (
        P(None, "rows", "cols", None),
        P(None, "rows", "cols", None),
        P(None, "rows", None, "cols", None),
        P(None, "rows", None),
        P(None, "rows"),
    )
    small = mesh.shape["rows"] == 16 and mesh.shape["cols"] == 2
    return jax.shard_map(
        local if small else local_any,
        mesh=mesh,
        in_specs=placed,
        out_specs=P(None, "rows", "cols", None),
        check_vma=False,
    )
```

```python
import functools

import jax
import jax.numpy as jnp
from jax import lax
from jax.experimental import pallas as pl
from jax.experimental.pallas import tpu as pltpu
from jax.sharding import PartitionSpec as P

KDEV = 7


def from_behind(value, axis, steps):
    count = lax.axis_size(axis)
    leading, last = (max(0, -steps), min(count, count - steps))
    return lax.ppermute(value, axis, [(source, source + steps) for source in range(leading, last)])


def local_any(rhs, diag_inv, factor_tiles, tile_source, tile_count):
    levels = rhs.shape[0]
    owned_count = rhs.shape[1]
    share_rows = rhs.shape[2]
    columns = rhs.shape[3]
    slot_count = tile_source.shape[2]
    reach_dev = KDEV
    window_len = 2 * reach_dev + 1
    total_sup = lax.axis_size("rows") * owned_count
    row_place = lax.axis_index("rows")
    highest = lax.Precision.HIGHEST
    slot_ids = jnp.arange(slot_count, dtype=jnp.int32)

    def window_places(sources):
        src_level = sources // total_sup
        within = sources % total_sup
        return (
            src_level * window_len + within // owned_count - row_place + reach_dev
        ) * owned_count + within % owned_count

    def live_mask(counts):
        return (slot_ids[None, :] < counts[:, None]).astype(jnp.float32)

    def full_rows(piece):
        return lax.all_gather(piece, "cols", axis=1, tiled=True)

    forward_values = []
    windows = []
    for height in range(levels):
        if height == 0:
            whole_block = full_rows(rhs[0])
        else:
            stacked = jnp.stack(windows, 0).reshape(
                height * window_len * owned_count, share_rows, columns
            )
            places = window_places(tile_source[height - 1])
            picked = (
                jnp.take(stacked, places, axis=0)
                * live_mask(tile_count[height - 1])[:, :, None, None]
            )
            partial_value = jnp.einsum(
                "skci,skcr->sir", factor_tiles[height - 1], picked, precision=highest
            )
            whole_block = full_rows(
                rhs[height]
                - lax.psum_scatter(partial_value, "cols", scatter_dimension=1, tiled=True)
            )
        values = jnp.einsum("sci,sir->scr", diag_inv[height], whole_block, precision=highest)
        forward_values.append(values)
        if height + 1 < levels:
            pieces = []
            for pull_offset in range(-reach_dev, reach_dev + 1):
                if pull_offset == 0:
                    pieces.append(values)
                else:
                    pieces.append(from_behind(values, "rows", -pull_offset))
            windows.append(jnp.stack(pieces, 0))
    carried = [jnp.zeros_like(forward_values[0]) for height in range(levels)]
    solution = [None] * levels
    for height in reversed(range(levels)):
        partial_value = jnp.einsum(
            "sci,scr->sir",
            diag_inv[height],
            forward_values[height] - carried[height],
            precision=highest,
        )
        own_share = lax.psum_scatter(partial_value, "cols", scatter_dimension=1, tiled=True)
        if height > 0:
            whole_block = lax.all_gather(own_share, "cols", axis=1, tiled=True)
        solution[height] = own_share
        if height > 0:
            term_set = jnp.einsum(
                "skci,sir->skcr", factor_tiles[height - 1], whole_block, precision=highest
            )
            term_set = term_set * live_mask(tile_count[height - 1])[:, :, None, None]
            places = window_places(tile_source[height - 1]).reshape(-1)
            targets = height * window_len * owned_count
            one_hot = (jnp.arange(targets, dtype=jnp.int32)[:, None] == places[None, :]).astype(
                jnp.float32
            )
            outgoing = jnp.einsum(
                "ms,slg->mlg",
                one_hot,
                term_set.reshape(owned_count * slot_count, share_rows, columns),
                precision=highest,
            )
            push_outgoing = outgoing.reshape(height, window_len, owned_count, share_rows, columns)
            received = push_outgoing[:, reach_dev]
            for offset in range(-reach_dev, reach_dev + 1):
                if offset != 0:
                    received = received + from_behind(
                        push_outgoing[:, reach_dev + offset], "rows", offset
                    )
            for lower_level in range(height):
                carried[lower_level] = carried[lower_level] + received[lower_level]
    return jnp.stack(solution, 0)


F32 = jnp.float32
BF16 = jnp.bfloat16
NN = (((1,), (0,)), ((), ()))
NT = (((1,), (1,)), ((), ()))
PIECES = 8


def halves(value):
    high = value.astype(BF16)
    return high, (value - high.astype(F32)).astype(BF16)


def dot3(left, right, dims):
    left_high, left_low = left if isinstance(left, tuple) else halves(left)
    right_high, right_low = right if isinstance(right, tuple) else halves(right)
    dot = functools.partial(lax.dot_general, dimension_numbers=dims, preferred_element_type=F32)
    rows = left_high.shape[0]
    both = dot(jnp.concatenate([left_high, left_low], 0), right_high)
    return both[:rows] + both[rows:] + dot(left_high, right_low)


def ordered(mine, theirs, place, axis):
    first = jnp.where(place == 0, mine, theirs)
    second = jnp.where(place == 0, theirs, mine)
    return jnp.concatenate([first, second], axis)


VMEM_LIMIT = 20 * 1024 * 1024


def options(cost):
    return dict(
        cost_estimate=pl.CostEstimate(flops=cost * 1000000, bytes_accessed=0, transcendentals=0),
        compiler_params=pltpu.CompilerParams(vmem_limit_bytes=VMEM_LIMIT),
    )


def call(kernel, name, outs, args, scalars=1, scratch=(), cost=1000):
    in_specs = [pl.BlockSpec(memory_space=pltpu.SMEM)] * scalars
    in_specs += [pl.BlockSpec(memory_space=pltpu.VMEM)] * (len(args) - scalars)
    return pl.pallas_call(
        kernel,
        out_shape=[
            jax.ShapeDtypeStruct(*out) if isinstance(out[0], tuple) else jax.ShapeDtypeStruct(out, F32)
            for out in outs
        ],
        in_specs=in_specs,
        out_specs=[pl.BlockSpec(memory_space=pltpu.VMEM)] * len(outs),
        scratch_shapes=list(scratch),
        name=name,
        **options(cost),
    )(*args)


def put_halves(value, high_out, low_out, at):
    high, low = halves(value)
    high_out[at] = high
    low_out[at] = low


def split_kernel(own, partner, *outs):
    put_halves(own[0, 0].reshape(-1, own.shape[-1]), *outs[:2], 0)
    put_halves(partner[0, 0].reshape(-1, own.shape[-1]), *outs[2:], 0)


def split_tiles(level, own, partner):
    own = pltpu.with_memory_space_constraint(own, pltpu.HBM)
    owned, slots, depth, width = own.shape[1:]
    block_in = pl.BlockSpec((1, 1, slots, depth, width), lambda s: (level, s, 0, 0, 0))
    block_out = pl.BlockSpec((1, slots * depth, width), lambda s: (s, 0, 0))
    return pl.pallas_call(
        split_kernel,
        grid=(owned,),
        out_shape=[jax.ShapeDtypeStruct((owned, slots * depth, width), BF16)] * 4,
        in_specs=[block_in] * 2,
        out_specs=[block_out] * 4,
        name="split_tiles",
        **options(2000),
    )(own, partner)


def whole_diag(level, diags, s):
    own, partner, own_other, partner_other = diags
    half = own.shape[1]
    if s < half:
        pair = own[level, s], own_other[level - 1, s]
    else:
        pair = partner[level, s % half], partner_other[level - 1, s % half]
    return jnp.concatenate(pair, 0)


def diag_by_tiles(d0, d1, d2, d3, *refs):
    tiles, outs = refs[:4], refs[4:]
    half = d0.shape[1]
    for s in range(2 * half):
        value = dot3(whole_diag(1, (d0, d1, d2, d3), s), part_of(tiles, s), NT)
        put_halves(value, *(outs[:2] if s < half else outs[2:]), s % half)


def gram_by_tiles(d0, d1, d2, d3, *refs):
    tiles, grams, outs = refs[:4], refs[4], refs[5:]
    half = d0.shape[1]
    for s in range(2 * half):
        diag = whole_diag(2, (d0, d1, d2, d3), s)
        gram = dot3(diag.T, diag, NN)
        grams[s] = gram
        value = dot3(gram, part_of(tiles, s), NT)
        put_halves(value, *(outs[:2] if s < half else outs[2:]), s % half)


def part_of(parts, s):
    count = len(parts) // 2
    half = parts[0].shape[0]
    chosen = parts[:count] if s < half else parts[count:]
    return tuple(part[s % half] for part in chosen)


def split_first(diag, high, low):
    for s in range(high.shape[0]):
        put_halves(diag[0, s], high, low, s)


def first_values(rhs_own, rhs_other, diag_high, diag_low, mine, partner):
    core, col = lax.axis_index("rows") % 2, lax.axis_index("cols")
    half = mine.shape[1]
    for s in range(rhs_own.shape[0]):
        rows = ordered(rhs_own[s], rhs_other[s], col, 0)
        values = dot3((diag_high[s], diag_low[s]), rows, NN).T
        low, high = values[:half], values[half:]
        mine[s] = jnp.where(core == 0, low, high)
        partner[s] = jnp.where(core == 0, high, low)


def split_diag(diag):
    shape = diag.shape[1:]
    return pl.pallas_call(
        split_first,
        grid=(1,),
        out_shape=[jax.ShapeDtypeStruct(shape, BF16)] * 2,
        in_specs=[pl.BlockSpec((1,) + shape, lambda i: (0, 0, 0, 0))],
        out_specs=[pl.BlockSpec(shape, lambda i: (0, 0, 0))] * 2,
        name="split_diag",
        **options(500),
    )(pltpu.with_memory_space_constraint(diag, pltpu.HBM))


def slot_places(sources, counts, places):
    row = lax.axis_index("rows")
    levels, owned, slots = sources.shape
    total = lax.axis_size("rows") * owned
    for l in range(levels):
        for s in range(owned):
            for k in range(slots):
                source = sources[l, s, k]
                live = k < counts[l, s]
                lower = jnp.where(source >= total, 1, 0)
                within = source - lower * total
                place = (row ^ (within // owned)) * owned + within % owned
                at = s * slots + k
                if l == 0:
                    places[0, at] = jnp.where(live, place, -1)
                else:
                    places[1, at] = jnp.where(live & (lower == 0), place, -1)
                    places[2, at] = jnp.where(live & (lower == 1), place, -1)


def place_of(places, index, slot, owned):
    own, partner = places
    count = own.shape[1]
    if slot < count:
        place = own[index, slot]
        return jnp.maximum(place, 0), place >= 0
    place = partner[index, slot - count]
    return jnp.where(place >= 0, place ^ owned, 0), place >= 0


def turned_rhs(rhs, mine, partner):
    core = lax.axis_index("rows") % 2
    half = mine.shape[2]
    for l in range(mine.shape[0]):
        for s in range(mine.shape[1]):
            rows = rhs[l + 1, s].T
            low, high = rows[:half], rows[half:]
            mine[l, s] = jnp.where(core == 0, low, high)
            partner[l, s] = jnp.where(core == 0, high, low)


def gathered(index, places, pieces, window):
    sups = pieces[0].shape[0]
    slots = 2 * places[0].shape[1] // sups
    for number, piece in enumerate(pieces):
        window[number * sups : (number + 1) * sups] = piece[...]
    for s in range(sups):
        picked = []
        for k in range(slots):
            place, live = place_of(places, index, s * slots + k, sups // 2)
            picked.append(jnp.where(live, window[place], 0.0))
        yield jnp.concatenate(picked, 1)


def upper_of(level, mine, partner, s):
    half = mine.shape[1]
    return mine[level - 1, s] if s < half else partner[level - 1, s % half]


def update_lower(index, level, places, places_partner, rhs, rhs_partner, *refs):
    tiles, pieces, (out, window) = refs[:4], refs[4:-2], refs[-2:]
    col = lax.axis_index("cols")
    for s, left in enumerate(gathered(index, (places, places_partner), pieces, window)):
        right = upper_of(level, rhs, rhs_partner, s)
        zero = jnp.zeros_like(right)
        base = jnp.concatenate([jnp.where(col == 0, right, zero), jnp.where(col == 0, zero, right)], 1)
        out[s] = base - dot3(left, part_of(tiles, s), NN)


def middle_values(residual, d0, d1, d2, d3, own, other):
    depth = own.shape[2]
    for s in range(own.shape[0]):
        values = dot3(residual[s], whole_diag(1, (d0, d1, d2, d3), s), NT)
        own[s] = values[:, :depth]
        other[s] = values[:, depth:]


def update_top(places, places_partner, *refs):
    tiles, base, pieces, (out, window) = refs[:4], refs[4], refs[5:-2], refs[-2:]
    for s, left in enumerate(gathered(2, (places, places_partner), pieces, window)):
        out[s] = base[s] - dot3(left, part_of(tiles, s), NN)


def add_terms(index, places, tiles, left, s, totals):
    owned = tiles[0].shape[0]
    depth = totals.shape[2]
    terms = dot3(left, part_of(tiles, s), NN)
    slots = terms.shape[1] // depth
    for k in range(slots):
        place, live = place_of(places, index, s * slots + k, owned)
        term = jnp.where(live, terms[:, k * depth : (k + 1) * depth], 0.0)
        totals[place] = totals[place] + term


def share_out(col, x, s, solved_mine, solved_partner):
    depth = solved_mine.shape[2]
    half = solved_mine.shape[0]
    share = jnp.where(col == 0, x[:, :depth], x[:, depth:])
    if s < half:
        solved_mine[s] = share
    else:
        solved_partner[s % half] = share


def pieces_out(totals, outs):
    first = 0
    for out in outs:
        out[...] = totals[first : first + out.shape[0]]
        first += out.shape[0]


def top_carry(places, places_partner, mine, theirs, t0, t1, t2, t3, residual, *rest):
    outs, totals = rest[:-1], rest[-1]
    totals[...] = jnp.zeros_like(totals)
    for s in range(residual.shape[0]):
        left = mine[s] + theirs[s]
        residual[s] = left
        add_terms(2, (places, places_partner), (t0, t1, t2, t3), left, s, totals)
    pieces_out(totals, outs)


def lowest_carry(
    places, places_partner, residual, t0, t1, t2, t3, grams,
    totals, solved_mine, solved_partner,
):
    totals[...] = jnp.zeros_like(totals)
    col = lax.axis_index("cols")
    for s in range(residual.shape[0]):
        share_out(col, dot3(residual[s], grams[s], NN), s, solved_mine, solved_partner)
        add_terms(1, (places, places_partner), (t0, t1, t2, t3), residual[s], s, totals)


def middle_carry(
    places, places_partner, own, other, d0, d1, d2, d3, t0, t1, t2, t3,
    lowest, solved_mine, solved_partner, *rest
):
    outs, totals = rest[:-1], rest[-1]
    totals[...] = lowest[...]
    for s in range(own.shape[0]):
        left = jnp.concatenate([own[s], other[s]], 1)
        add_terms(0, (places, places_partner), (t0, t1, t2, t3), left, s, totals)
        x = dot3(left, whole_diag(1, (d0, d1, d2, d3), s), NN)
        share_out(lax.axis_index("cols"), x, s, solved_mine, solved_partner)
    pieces_out(totals, outs)


def last_product(values, a, b, c, d, e, d_own, d_partner, mine, partner):
    sups = values.shape[0]
    half = sups // 2
    for s in range(sups):
        carried = a[s] + b[s] + c[s] + d[s] + e[s]
        diag, out = (d_own, mine) if s < half else (d_partner, partner)
        out[s % half] = dot3(values[s] - carried, diag[0, s % half], NN)


def turned_solution(mine, partner, own, other):
    core, col = lax.axis_index("rows") % 2, lax.axis_index("cols")
    depth = own.shape[1]
    for s in range(mine.shape[0]):
        both = ordered(mine[s], partner[s], core, 0)
        low, high = both[:, :depth].T, both[:, depth:].T
        own[s] = jnp.where(col == 0, low, high)
        other[s] = jnp.where(col == 0, high, low)


def turned_upper(mine2, partner2, mine1, partner1, out):
    core = lax.axis_index("rows") % 2
    for s in range(mine2.shape[0]):
        out[0, s] = ordered(mine1[s], partner1[s], core, 0).T
        out[1, s] = ordered(mine2[s], partner2[s], core, 0).T


def local(rhs, diag_inv, factor_tiles, tile_source, tile_count):
    levels, owned, share_rows, columns = rhs.shape
    slots = tile_source.shape[2]
    sups = 2 * owned
    block = share_rows * 2
    half_columns = columns // 2
    rows_total = lax.axis_size("rows")
    piece = (sups, half_columns, share_rows)
    shared = (owned, half_columns, share_rows)
    window = (PIECES * sups, half_columns, share_rows)
    after = lax.optimization_barrier

    def swap_cols(value):
        return lax.ppermute(value, "cols", [(0, 1), (1, 0)])

    def swap_rows(value, bits):
        return lax.ppermute(value, "rows", [(r, r ^ bits) for r in range(rows_total)])

    def swap_core(value):
        return swap_rows(value, 1)

    def swap_x(value):
        return swap_rows(value, 2)

    def swap_mid(value):
        low, high = rows_total // 4, 3 * rows_total // 4
        pairs = [(r, r ^ 12 if low <= r < high else r ^ 2) for r in range(rows_total)]
        return lax.ppermute(value, "rows", pairs)

    def gather_pieces(value):
        far = swap_rows(value, 8)
        beside = swap_x(value)
        mid = swap_mid(value)
        near = swap_rows(value, 4)
        return [
            value, beside, near, swap_rows(beside, 4), far, swap_x(far), mid, swap_mid(beside)
        ]

    def scatter_upper(p):
        far = swap_rows(p[4] + swap_x(p[5]), 8)
        beside = swap_x(p[1] + (swap_mid(p[7]) + swap_rows(p[3], 4)))
        mid = swap_mid(p[6])
        near = swap_rows(p[2], 4)
        return [p[0], far, beside, mid, near]

    def scatter_lowest(p):
        far = swap_rows(p[4] + swap_x(p[5]), 8)
        beside = swap_x(p[1] + (swap_mid(p[7]) + swap_rows(p[3], 4)))
        mid = swap_mid(p[6])
        near = swap_rows(p[2], 4)
        return [p[0], near, mid, beside, far]

    rhs0 = rhs[0]
    rhs0_other = swap_cols(rhs0)
    d_partner = swap_core(diag_inv)
    tiles_partner = swap_core(factor_tiles)
    d_low = split_diag(diag_inv)
    upper_diag = diag_inv[1:]
    d_other = swap_cols(upper_diag)
    tile_source, upper_diag, rhs0 = after((tile_source, upper_diag, rhs0))
    own_places = pl.pallas_call(
        slot_places,
        out_shape=jax.ShapeDtypeStruct((levels, owned * slots), jnp.int32),
        in_specs=[pl.BlockSpec(memory_space=pltpu.SMEM)] * 2,
        out_specs=pl.BlockSpec(memory_space=pltpu.SMEM),
        name="slot_places",
        **options(500),
    )(tile_source, tile_count)
    places = [own_places, swap_core(own_places)]
    rhs0, places, tiles_partner, d_partner, d_low = after(
        (rhs0, places, tiles_partner, d_partner, d_low)
    )
    mine, partner = call(first_values, "first_values", [shared] * 2, [rhs0, rhs0_other, *d_low], 0)
    values0 = jnp.concatenate([mine, swap_core(partner)], 0)
    upper, upper_partner = call(
        turned_rhs, "turned_rhs", [(levels - 1, owned, half_columns, share_rows)] * 2, [rhs], 0
    )
    uppers = [upper, swap_core(upper_partner)]
    values0, uppers = after((values0, uppers))
    pieces0 = gather_pieces(values0)

    reach = slots * share_rows
    wide = [((owned, block, reach), BF16)] * 4
    low_tiles = split_tiles(0, factor_tiles, tiles_partner)
    full = (sups, half_columns, block)
    scratch = [pltpu.VMEM(window, F32)]
    d_other, _ = after((d_other, (low_tiles, uppers, pieces0)))
    diags = [diag_inv, d_partner, d_other, swap_core(d_other)]
    partial = call(
        functools.partial(update_lower, 0, 1), "update_middle", [full],
        [*places, *uppers, *low_tiles, *pieces0], 2, scratch,
    )[0]
    own, other = call(middle_values, "middle_values", [piece] * 2, [partial, *diags], 0)
    values1 = own + swap_cols(other)
    pieces1 = gather_pieces(values1)
    tiles, _ = after((factor_tiles, values1))
    top_tiles = split_tiles(1, tiles, tiles_partner)
    base = call(
        functools.partial(update_lower, 1, 2), "update_top_low", [full],
        [*places, *uppers, *top_tiles, *pieces0], 2, scratch,
    )[0]

    partial = call(
        update_top, "update_top", [full], [*places, *top_tiles, base, *pieces1], 2, scratch
    )[0]
    top_ready, _ = after((top_tiles, partial))
    grams, *top_turned = call(
        gram_by_tiles, "gram_by_tiles", [(sups, block, block)] + wide, [*diags, *top_ready], 0,
        cost=3000,
    )
    residual, *out = call(
        top_carry, "top_carry", [full] + [piece] * PIECES,
        [*places, partial, swap_cols(partial), *top_turned], 2, scratch,
    )
    carried = values1 - functools.reduce(jnp.add, scatter_upper(out))
    residual, low_ready, _ = after((residual, low_tiles, carried))
    low_turned = call(diag_by_tiles, "diag_by_tiles", wide, [*diags, *low_ready], 0, cost=3000)
    lowest, mine2, partner2 = call(
        lowest_carry, "lowest_carry", [window, shared, shared],
        [*places, residual, *top_turned, grams], 2, cost=2000,
    )

    mine1, partner1, *out = call(
        middle_carry, "middle_carry", [shared, shared] + [piece] * PIECES,
        [*places, carried, swap_cols(carried), *diags, *low_turned, lowest],
        2, scratch,
    )

    mine, partner = call(
        last_product, "last_product", [(owned, half_columns, block)] * 2,
        [values0, *scatter_lowest(out), diag_inv, d_partner], 0,
    )
    own, other = call(
        turned_solution, "turned_solution", [(owned, share_rows, columns)] * 2,
        [mine, swap_core(partner)], 0,
    )
    own = own + swap_cols(other)

    partner1, partner2, _ = after((partner1, partner2, mine))
    result_upper = call(
        turned_upper, "turned_upper", [(levels - 1, owned, share_rows, columns)],
        [mine2, swap_core(partner2), mine1, swap_core(partner1)], 0,
    )[0]
    return jnp.concatenate([own[None], result_upper], 0)


def solution(mesh):
    placed = (
        P(None, "rows", "cols", None),
        P(None, "rows", "cols", None),
        P(None, "rows", None, "cols", None),
        P(None, "rows", None),
        P(None, "rows"),
    )
    small = mesh.shape["rows"] == 16 and mesh.shape["cols"] == 2
    return jax.shard_map(
        local if small else local_any,
        mesh=mesh,
        in_specs=placed,
        out_specs=P(None, "rows", "cols", None),
        check_vma=False,
    )
```

```python
import functools

import jax
import jax.numpy as jnp
from jax import lax
from jax.experimental import pallas as pl
from jax.experimental.pallas import tpu as pltpu
from jax.sharding import PartitionSpec as P

KDEV = 7


def from_behind(value, axis, steps):
    count = lax.axis_size(axis)
    leading, last = (max(0, -steps), min(count, count - steps))
    return lax.ppermute(value, axis, [(source, source + steps) for source in range(leading, last)])


def local_any(rhs, diag_inv, factor_tiles, tile_source, tile_count):
    levels = rhs.shape[0]
    owned_count = rhs.shape[1]
    share_rows = rhs.shape[2]
    columns = rhs.shape[3]
    slot_count = tile_source.shape[2]
    reach_dev = KDEV
    window_len = 2 * reach_dev + 1
    total_sup = lax.axis_size("rows") * owned_count
    row_place = lax.axis_index("rows")
    highest = lax.Precision.HIGHEST
    slot_ids = jnp.arange(slot_count, dtype=jnp.int32)

    def window_places(sources):
        src_level = sources // total_sup
        within = sources % total_sup
        return (
            src_level * window_len + within // owned_count - row_place + reach_dev
        ) * owned_count + within % owned_count

    def live_mask(counts):
        return (slot_ids[None, :] < counts[:, None]).astype(jnp.float32)

    def full_rows(piece):
        return lax.all_gather(piece, "cols", axis=1, tiled=True)

    forward_values = []
    windows = []
    for height in range(levels):
        if height == 0:
            whole_block = full_rows(rhs[0])
        else:
            stacked = jnp.stack(windows, 0).reshape(
                height * window_len * owned_count, share_rows, columns
            )
            places = window_places(tile_source[height - 1])
            picked = (
                jnp.take(stacked, places, axis=0)
                * live_mask(tile_count[height - 1])[:, :, None, None]
            )
            partial_value = jnp.einsum(
                "skci,skcr->sir", factor_tiles[height - 1], picked, precision=highest
            )
            whole_block = full_rows(
                rhs[height]
                - lax.psum_scatter(partial_value, "cols", scatter_dimension=1, tiled=True)
            )
        values = jnp.einsum("sci,sir->scr", diag_inv[height], whole_block, precision=highest)
        forward_values.append(values)
        if height + 1 < levels:
            pieces = []
            for pull_offset in range(-reach_dev, reach_dev + 1):
                if pull_offset == 0:
                    pieces.append(values)
                else:
                    pieces.append(from_behind(values, "rows", -pull_offset))
            windows.append(jnp.stack(pieces, 0))
    carried = [jnp.zeros_like(forward_values[0]) for height in range(levels)]
    solution = [None] * levels
    for height in reversed(range(levels)):
        partial_value = jnp.einsum(
            "sci,scr->sir",
            diag_inv[height],
            forward_values[height] - carried[height],
            precision=highest,
        )
        own_share = lax.psum_scatter(partial_value, "cols", scatter_dimension=1, tiled=True)
        if height > 0:
            whole_block = lax.all_gather(own_share, "cols", axis=1, tiled=True)
        solution[height] = own_share
        if height > 0:
            term_set = jnp.einsum(
                "skci,sir->skcr", factor_tiles[height - 1], whole_block, precision=highest
            )
            term_set = term_set * live_mask(tile_count[height - 1])[:, :, None, None]
            places = window_places(tile_source[height - 1]).reshape(-1)
            targets = height * window_len * owned_count
            one_hot = (jnp.arange(targets, dtype=jnp.int32)[:, None] == places[None, :]).astype(
                jnp.float32
            )
            outgoing = jnp.einsum(
                "ms,slg->mlg",
                one_hot,
                term_set.reshape(owned_count * slot_count, share_rows, columns),
                precision=highest,
            )
            push_outgoing = outgoing.reshape(height, window_len, owned_count, share_rows, columns)
            received = push_outgoing[:, reach_dev]
            for offset in range(-reach_dev, reach_dev + 1):
                if offset != 0:
                    received = received + from_behind(
                        push_outgoing[:, reach_dev + offset], "rows", offset
                    )
            for lower_level in range(height):
                carried[lower_level] = carried[lower_level] + received[lower_level]
    return jnp.stack(solution, 0)


F32 = jnp.float32
BF16 = jnp.bfloat16
NN = (((1,), (0,)), ((), ()))
NT = (((1,), (1,)), ((), ()))
PIECES = 8


def halves(value):
    high = value.astype(BF16)
    return high, (value - high.astype(F32)).astype(BF16)


def dot3(left, right, dims):
    left_high, left_low = left if isinstance(left, tuple) else halves(left)
    right_high, right_low = right if isinstance(right, tuple) else halves(right)
    dot = functools.partial(lax.dot_general, dimension_numbers=dims, preferred_element_type=F32)
    rows = left_high.shape[0]
    both = dot(jnp.concatenate([left_high, left_low], 0), right_high)
    return both[:rows] + both[rows:] + dot(left_high, right_low)


def ordered(mine, theirs, place, axis):
    first = jnp.where(place == 0, mine, theirs)
    second = jnp.where(place == 0, theirs, mine)
    return jnp.concatenate([first, second], axis)


VMEM_LIMIT = 20 * 1024 * 1024


def options(cost):
    return dict(
        cost_estimate=pl.CostEstimate(flops=cost * 1000000, bytes_accessed=0, transcendentals=0),
        compiler_params=pltpu.CompilerParams(vmem_limit_bytes=VMEM_LIMIT),
    )


def call(kernel, name, outs, args, scalars=1, scratch=(), cost=1000):
    in_specs = [pl.BlockSpec(memory_space=pltpu.SMEM)] * scalars
    in_specs += [pl.BlockSpec(memory_space=pltpu.VMEM)] * (len(args) - scalars)
    return pl.pallas_call(
        kernel,
        out_shape=[
            jax.ShapeDtypeStruct(*out) if isinstance(out[0], tuple) else jax.ShapeDtypeStruct(out, F32)
            for out in outs
        ],
        in_specs=in_specs,
        out_specs=[pl.BlockSpec(memory_space=pltpu.VMEM)] * len(outs),
        scratch_shapes=list(scratch),
        name=name,
        **options(cost),
    )(*args)


def put_halves(value, high_out, low_out, at):
    high, low = halves(value)
    high_out[at] = high
    low_out[at] = low


def split_kernel(own, partner, *outs):
    put_halves(own[0, 0].reshape(-1, own.shape[-1]), *outs[:2], 0)
    put_halves(partner[0, 0].reshape(-1, own.shape[-1]), *outs[2:], 0)


def split_tiles(level, own, partner):
    own = pltpu.with_memory_space_constraint(own, pltpu.HBM)
    owned, slots, depth, width = own.shape[1:]
    block_in = pl.BlockSpec((1, 1, slots, depth, width), lambda s: (level, s, 0, 0, 0))
    block_out = pl.BlockSpec((1, slots * depth, width), lambda s: (s, 0, 0))
    return pl.pallas_call(
        split_kernel,
        grid=(owned,),
        out_shape=[jax.ShapeDtypeStruct((owned, slots * depth, width), BF16)] * 4,
        in_specs=[block_in] * 2,
        out_specs=[block_out] * 4,
        name="split_tiles",
        **options(2000),
    )(own, partner)


def whole_diag(level, diags, s):
    own, partner, own_other, partner_other = diags
    half = own.shape[1]
    if s < half:
        pair = own[level, s], own_other[level - 1, s]
    else:
        pair = partner[level, s % half], partner_other[level - 1, s % half]
    return jnp.concatenate(pair, 0)


def diag_by_tiles(d0, d1, d2, d3, *refs):
    tiles, outs = refs[:4], refs[4:]
    half = d0.shape[1]
    for s in range(2 * half):
        value = dot3(whole_diag(1, (d0, d1, d2, d3), s), part_of(tiles, s), NT)
        put_halves(value, *(outs[:2] if s < half else outs[2:]), s % half)


def gram_by_tiles(d0, d1, d2, d3, *refs):
    tiles, grams, outs = refs[:4], refs[4], refs[5:]
    half = d0.shape[1]
    for s in range(2 * half):
        diag = whole_diag(2, (d0, d1, d2, d3), s)
        gram = dot3(diag.T, diag, NN)
        grams[s] = gram
        value = dot3(gram, part_of(tiles, s), NT)
        put_halves(value, *(outs[:2] if s < half else outs[2:]), s % half)


def part_of(parts, s):
    count = len(parts) // 2
    half = parts[0].shape[0]
    chosen = parts[:count] if s < half else parts[count:]
    return tuple(part[s % half] for part in chosen)


def split_first(diag, high, low):
    for s in range(high.shape[0]):
        put_halves(diag[0, s], high, low, s)


def first_values(rhs_own, rhs_other, diag_high, diag_low, mine, partner):
    core, col = lax.axis_index("rows") % 2, lax.axis_index("cols")
    half = mine.shape[1]
    for s in range(rhs_own.shape[0]):
        rows = ordered(rhs_own[s], rhs_other[s], col, 0)
        values = dot3((diag_high[s], diag_low[s]), rows, NN).T
        low, high = values[:half], values[half:]
        mine[s] = jnp.where(core == 0, low, high)
        partner[s] = jnp.where(core == 0, high, low)


def split_diag(diag):
    shape = diag.shape[1:]
    return pl.pallas_call(
        split_first,
        grid=(1,),
        out_shape=[jax.ShapeDtypeStruct(shape, BF16)] * 2,
        in_specs=[pl.BlockSpec((1,) + shape, lambda i: (0, 0, 0, 0))],
        out_specs=[pl.BlockSpec(shape, lambda i: (0, 0, 0))] * 2,
        name="split_diag",
        **options(500),
    )(pltpu.with_memory_space_constraint(diag, pltpu.HBM))


def slot_places(sources, counts, places):
    row = lax.axis_index("rows")
    levels, owned, slots = sources.shape
    total = lax.axis_size("rows") * owned
    for l in range(levels):
        for s in range(owned):
            for k in range(slots):
                source = sources[l, s, k]
                live = k < counts[l, s]
                lower = jnp.where(source >= total, 1, 0)
                within = source - lower * total
                place = (row ^ (within // owned)) * owned + within % owned
                at = s * slots + k
                if l == 0:
                    places[0, at] = jnp.where(live, place, -1)
                else:
                    places[1, at] = jnp.where(live & (lower == 0), place, -1)
                    places[2, at] = jnp.where(live & (lower == 1), place, -1)


def place_of(places, index, slot, owned):
    own, partner = places
    count = own.shape[1]
    if slot < count:
        place = own[index, slot]
        return jnp.maximum(place, 0), place >= 0
    place = partner[index, slot - count]
    return jnp.where(place >= 0, place ^ owned, 0), place >= 0


def turned_rhs(rhs, mine, partner):
    core = lax.axis_index("rows") % 2
    half = mine.shape[2]
    for l in range(mine.shape[0]):
        for s in range(mine.shape[1]):
            rows = rhs[l + 1, s].T
            low, high = rows[:half], rows[half:]
            mine[l, s] = jnp.where(core == 0, low, high)
            partner[l, s] = jnp.where(core == 0, high, low)


def gathered(index, places, pieces, window):
    sups = pieces[0].shape[0]
    slots = 2 * places[0].shape[1] // sups
    for number, piece in enumerate(pieces):
        window[number * sups : (number + 1) * sups] = piece[...]
    for s in range(sups):
        picked = []
        for k in range(slots):
            place, live = place_of(places, index, s * slots + k, sups // 2)
            picked.append(jnp.where(live, window[place], 0.0))
        yield jnp.concatenate(picked, 1)


def upper_of(level, mine, partner, s):
    half = mine.shape[1]
    return mine[level - 1, s] if s < half else partner[level - 1, s % half]


def update_lower(index, level, places, places_partner, rhs, rhs_partner, *refs):
    tiles, pieces, (out, window) = refs[:4], refs[4:-2], refs[-2:]
    col = lax.axis_index("cols")
    for s, left in enumerate(gathered(index, (places, places_partner), pieces, window)):
        right = upper_of(level, rhs, rhs_partner, s)
        zero = jnp.zeros_like(right)
        base = jnp.concatenate([jnp.where(col == 0, right, zero), jnp.where(col == 0, zero, right)], 1)
        out[s] = base - dot3(left, part_of(tiles, s), NN)


def middle_values(residual, d0, d1, d2, d3, own, other):
    depth = own.shape[2]
    for s in range(own.shape[0]):
        values = dot3(residual[s], whole_diag(1, (d0, d1, d2, d3), s), NT)
        own[s] = values[:, :depth]
        other[s] = values[:, depth:]


def update_top(places, places_partner, *refs):
    tiles, base, pieces, (out, window) = refs[:4], refs[4], refs[5:-2], refs[-2:]
    for s, left in enumerate(gathered(2, (places, places_partner), pieces, window)):
        out[s] = base[s] - dot3(left, part_of(tiles, s), NN)


def add_terms(index, places, tiles, left, s, totals):
    owned = tiles[0].shape[0]
    depth = totals.shape[2]
    terms = dot3(left, part_of(tiles, s), NN)
    slots = terms.shape[1] // depth
    for k in range(slots):
        place, live = place_of(places, index, s * slots + k, owned)
        term = jnp.where(live, terms[:, k * depth : (k + 1) * depth], 0.0)
        totals[place] = totals[place] + term


def share_out(col, x, s, solved_mine, solved_partner):
    depth = solved_mine.shape[2]
    half = solved_mine.shape[0]
    share = jnp.where(col == 0, x[:, :depth], x[:, depth:])
    if s < half:
        solved_mine[s] = share
    else:
        solved_partner[s % half] = share


def pieces_out(totals, outs):
    first = 0
    for out in outs:
        out[...] = totals[first : first + out.shape[0]]
        first += out.shape[0]


def top_carry(places, places_partner, mine, theirs, t0, t1, t2, t3, residual, *rest):
    outs, totals = rest[:-1], rest[-1]
    totals[...] = jnp.zeros_like(totals)
    for s in range(residual.shape[0]):
        left = mine[s] + theirs[s]
        residual[s] = left
        add_terms(2, (places, places_partner), (t0, t1, t2, t3), left, s, totals)
    pieces_out(totals, outs)


def lowest_carry(
    places, places_partner, residual, t0, t1, t2, t3, grams,
    totals, solved_mine, solved_partner,
):
    totals[...] = jnp.zeros_like(totals)
    col = lax.axis_index("cols")
    for s in range(residual.shape[0]):
        share_out(col, dot3(residual[s], grams[s], NN), s, solved_mine, solved_partner)
        add_terms(1, (places, places_partner), (t0, t1, t2, t3), residual[s], s, totals)


def middle_carry(
    places, places_partner, own, other, d0, d1, d2, d3, t0, t1, t2, t3,
    lowest, solved_mine, solved_partner, *rest
):
    outs, totals = rest[:-1], rest[-1]
    totals[...] = lowest[...]
    for s in range(own.shape[0]):
        left = jnp.concatenate([own[s], other[s]], 1)
        add_terms(0, (places, places_partner), (t0, t1, t2, t3), left, s, totals)
        x = dot3(left, whole_diag(1, (d0, d1, d2, d3), s), NN)
        share_out(lax.axis_index("cols"), x, s, solved_mine, solved_partner)
    pieces_out(totals, outs)


def last_product(values, a, b, c, d, e, d_own, d_partner, mine, partner):
    sups = values.shape[0]
    half = sups // 2
    for s in range(sups):
        carried = a[s] + b[s] + c[s] + d[s] + e[s]
        diag, out = (d_own, mine) if s < half else (d_partner, partner)
        out[s % half] = dot3(values[s] - carried, diag[0, s % half], NN)


def turned_solution(mine, partner, own, other):
    core, col = lax.axis_index("rows") % 2, lax.axis_index("cols")
    depth = own.shape[1]
    for s in range(mine.shape[0]):
        both = ordered(mine[s], partner[s], core, 0)
        low, high = both[:, :depth].T, both[:, depth:].T
        own[s] = jnp.where(col == 0, low, high)
        other[s] = jnp.where(col == 0, high, low)


def turned_upper(mine2, partner2, mine1, partner1, out):
    core = lax.axis_index("rows") % 2
    for s in range(mine2.shape[0]):
        out[0, s] = ordered(mine1[s], partner1[s], core, 0).T
        out[1, s] = ordered(mine2[s], partner2[s], core, 0).T


def local(rhs, diag_inv, factor_tiles, tile_source, tile_count):
    levels, owned, share_rows, columns = rhs.shape
    slots = tile_source.shape[2]
    sups = 2 * owned
    block = share_rows * 2
    half_columns = columns // 2
    rows_total = lax.axis_size("rows")
    piece = (sups, half_columns, share_rows)
    shared = (owned, half_columns, share_rows)
    window = (PIECES * sups, half_columns, share_rows)
    after = lax.optimization_barrier

    def swap_cols(value):
        return lax.ppermute(value, "cols", [(0, 1), (1, 0)])

    def swap_rows(value, bits):
        return lax.ppermute(value, "rows", [(r, r ^ bits) for r in range(rows_total)])

    def swap_core(value):
        return swap_rows(value, 1)

    def swap_x(value):
        return swap_rows(value, 2)

    def swap_mid(value):
        low, high = rows_total // 4, 3 * rows_total // 4
        pairs = [(r, r ^ 12 if low <= r < high else r ^ 2) for r in range(rows_total)]
        return lax.ppermute(value, "rows", pairs)

    def gather_pieces(value):
        far = swap_rows(value, 8)
        beside = swap_x(value)
        mid = swap_mid(value)
        near = swap_rows(value, 4)
        return [
            value, beside, near, swap_rows(beside, 4), far, swap_x(far), mid, swap_mid(beside)
        ]

    def scatter_upper(p):
        far = swap_rows(p[4] + swap_x(p[5]), 8)
        beside = swap_x(p[1] + (swap_mid(p[7]) + swap_rows(p[3], 4)))
        mid = swap_mid(p[6])
        near = swap_rows(p[2], 4)
        return [p[0], far, beside, mid, near]

    def scatter_lowest(p):
        far = swap_rows(p[4] + swap_x(p[5]), 8)
        beside = swap_x(p[1] + (swap_mid(p[7]) + swap_rows(p[3], 4)))
        mid = swap_mid(p[6])
        near = swap_rows(p[2], 4)
        return [p[0], near, mid, beside, far]

    rhs0 = rhs[0]
    rhs0_other = swap_cols(rhs0)
    d_partner = swap_core(diag_inv)
    tiles_partner = swap_core(factor_tiles)
    d_low = split_diag(diag_inv)
    upper_diag = diag_inv[1:]
    d_other = swap_cols(upper_diag)
    tile_source, upper_diag, rhs0 = after((tile_source, upper_diag, rhs0))
    own_places = pl.pallas_call(
        slot_places,
        out_shape=jax.ShapeDtypeStruct((levels, owned * slots), jnp.int32),
        in_specs=[pl.BlockSpec(memory_space=pltpu.SMEM)] * 2,
        out_specs=pl.BlockSpec(memory_space=pltpu.SMEM),
        name="slot_places",
        **options(500),
    )(tile_source, tile_count)
    places = [own_places, swap_core(own_places)]
    rhs0, places, tiles_partner, d_partner, d_low = after(
        (rhs0, places, tiles_partner, d_partner, d_low)
    )
    mine, partner = call(first_values, "first_values", [shared] * 2, [rhs0, rhs0_other, *d_low], 0)
    values0 = jnp.concatenate([mine, swap_core(partner)], 0)
    upper, upper_partner = call(
        turned_rhs, "turned_rhs", [(levels - 1, owned, half_columns, share_rows)] * 2, [rhs], 0
    )
    uppers = [upper, swap_core(upper_partner)]
    values0, uppers = after((values0, uppers))
    pieces0 = gather_pieces(values0)

    reach = slots * share_rows
    wide = [((owned, block, reach), BF16)] * 4
    low_tiles = split_tiles(0, factor_tiles, tiles_partner)
    full = (sups, half_columns, block)
    scratch = [pltpu.VMEM(window, F32)]
    d_other, _ = after((d_other, (low_tiles, uppers, pieces0)))
    diags = [diag_inv, d_partner, d_other, swap_core(d_other)]
    partial = call(
        functools.partial(update_lower, 0, 1), "update_middle", [full],
        [*places, *uppers, *low_tiles, *pieces0], 2, scratch,
    )[0]
    own, other = call(middle_values, "middle_values", [piece] * 2, [partial, *diags], 0)
    low_ready, _ = after((low_tiles, other))
    low_turned = call(diag_by_tiles, "diag_by_tiles", wide, [*diags, *low_ready], 0, cost=3000)
    own, low_turned = after((own, low_turned))
    values1 = own + swap_cols(other)
    pieces1 = gather_pieces(values1)
    tiles, _ = after((factor_tiles, values1))
    top_tiles = split_tiles(1, tiles, tiles_partner)
    base = call(
        functools.partial(update_lower, 1, 2), "update_top_low", [full],
        [*places, *uppers, *top_tiles, *pieces0], 2, scratch,
    )[0]

    partial = call(
        update_top, "update_top", [full], [*places, *top_tiles, base, *pieces1], 2, scratch
    )[0]
    top_ready, _ = after((top_tiles, partial))
    grams, *top_turned = call(
        gram_by_tiles, "gram_by_tiles", [(sups, block, block)] + wide, [*diags, *top_ready], 0,
        cost=3000,
    )
    residual, *out = call(
        top_carry, "top_carry", [full] + [piece] * PIECES,
        [*places, partial, swap_cols(partial), *top_turned], 2, scratch,
    )
    carried = values1 - functools.reduce(jnp.add, scatter_upper(out))
    residual, _ = after((residual, carried))
    lowest, mine2, partner2 = call(
        lowest_carry, "lowest_carry", [window, shared, shared],
        [*places, residual, *top_turned, grams], 2, cost=2000,
    )

    mine1, partner1, *out = call(
        middle_carry, "middle_carry", [shared, shared] + [piece] * PIECES,
        [*places, carried, swap_cols(carried), *diags, *low_turned, lowest],
        2, scratch,
    )

    mine, partner = call(
        last_product, "last_product", [(owned, half_columns, block)] * 2,
        [values0, *scatter_lowest(out), diag_inv, d_partner], 0,
    )
    own, other = call(
        turned_solution, "turned_solution", [(owned, share_rows, columns)] * 2,
        [mine, swap_core(partner)], 0,
    )
    own = own + swap_cols(other)

    partner1, partner2, _ = after((partner1, partner2, mine))
    result_upper = call(
        turned_upper, "turned_upper", [(levels - 1, owned, share_rows, columns)],
        [mine2, swap_core(partner2), mine1, swap_core(partner1)], 0,
    )[0]
    return jnp.concatenate([own[None], result_upper], 0)


def solution(mesh):
    placed = (
        P(None, "rows", "cols", None),
        P(None, "rows", "cols", None),
        P(None, "rows", None, "cols", None),
        P(None, "rows", None),
        P(None, "rows"),
    )
    small = mesh.shape["rows"] == 16 and mesh.shape["cols"] == 2
    return jax.shard_map(
        local if small else local_any,
        mesh=mesh,
        in_specs=placed,
        out_specs=P(None, "rows", "cols", None),
        check_vma=False,
    )
```

```python
import functools

import jax
import jax.numpy as jnp
from jax import lax
from jax.experimental import pallas as pl
from jax.experimental.pallas import tpu as pltpu
from jax.sharding import PartitionSpec as P

KDEV = 7


def from_behind(value, axis, steps):
    count = lax.axis_size(axis)
    leading, last = (max(0, -steps), min(count, count - steps))
    return lax.ppermute(value, axis, [(source, source + steps) for source in range(leading, last)])


def local_any(rhs, diag_inv, factor_tiles, tile_source, tile_count):
    levels = rhs.shape[0]
    owned_count = rhs.shape[1]
    share_rows = rhs.shape[2]
    columns = rhs.shape[3]
    slot_count = tile_source.shape[2]
    reach_dev = KDEV
    window_len = 2 * reach_dev + 1
    total_sup = lax.axis_size("rows") * owned_count
    row_place = lax.axis_index("rows")
    highest = lax.Precision.HIGHEST
    slot_ids = jnp.arange(slot_count, dtype=jnp.int32)

    def window_places(sources):
        src_level = sources // total_sup
        within = sources % total_sup
        return (
            src_level * window_len + within // owned_count - row_place + reach_dev
        ) * owned_count + within % owned_count

    def live_mask(counts):
        return (slot_ids[None, :] < counts[:, None]).astype(jnp.float32)

    def full_rows(piece):
        return lax.all_gather(piece, "cols", axis=1, tiled=True)

    forward_values = []
    windows = []
    for height in range(levels):
        if height == 0:
            whole_block = full_rows(rhs[0])
        else:
            stacked = jnp.stack(windows, 0).reshape(
                height * window_len * owned_count, share_rows, columns
            )
            places = window_places(tile_source[height - 1])
            picked = (
                jnp.take(stacked, places, axis=0)
                * live_mask(tile_count[height - 1])[:, :, None, None]
            )
            partial_value = jnp.einsum(
                "skci,skcr->sir", factor_tiles[height - 1], picked, precision=highest
            )
            whole_block = full_rows(
                rhs[height]
                - lax.psum_scatter(partial_value, "cols", scatter_dimension=1, tiled=True)
            )
        values = jnp.einsum("sci,sir->scr", diag_inv[height], whole_block, precision=highest)
        forward_values.append(values)
        if height + 1 < levels:
            pieces = []
            for pull_offset in range(-reach_dev, reach_dev + 1):
                if pull_offset == 0:
                    pieces.append(values)
                else:
                    pieces.append(from_behind(values, "rows", -pull_offset))
            windows.append(jnp.stack(pieces, 0))
    carried = [jnp.zeros_like(forward_values[0]) for height in range(levels)]
    solution = [None] * levels
    for height in reversed(range(levels)):
        partial_value = jnp.einsum(
            "sci,scr->sir",
            diag_inv[height],
            forward_values[height] - carried[height],
            precision=highest,
        )
        own_share = lax.psum_scatter(partial_value, "cols", scatter_dimension=1, tiled=True)
        if height > 0:
            whole_block = lax.all_gather(own_share, "cols", axis=1, tiled=True)
        solution[height] = own_share
        if height > 0:
            term_set = jnp.einsum(
                "skci,sir->skcr", factor_tiles[height - 1], whole_block, precision=highest
            )
            term_set = term_set * live_mask(tile_count[height - 1])[:, :, None, None]
            places = window_places(tile_source[height - 1]).reshape(-1)
            targets = height * window_len * owned_count
            one_hot = (jnp.arange(targets, dtype=jnp.int32)[:, None] == places[None, :]).astype(
                jnp.float32
            )
            outgoing = jnp.einsum(
                "ms,slg->mlg",
                one_hot,
                term_set.reshape(owned_count * slot_count, share_rows, columns),
                precision=highest,
            )
            push_outgoing = outgoing.reshape(height, window_len, owned_count, share_rows, columns)
            received = push_outgoing[:, reach_dev]
            for offset in range(-reach_dev, reach_dev + 1):
                if offset != 0:
                    received = received + from_behind(
                        push_outgoing[:, reach_dev + offset], "rows", offset
                    )
            for lower_level in range(height):
                carried[lower_level] = carried[lower_level] + received[lower_level]
    return jnp.stack(solution, 0)


F32 = jnp.float32
BF16 = jnp.bfloat16
NN = (((1,), (0,)), ((), ()))
NT = (((1,), (1,)), ((), ()))
PIECES = 8


def halves(value):
    high = value.astype(BF16)
    return high, (value - high.astype(F32)).astype(BF16)


def dot3(left, right, dims):
    left_high, left_low = left if isinstance(left, tuple) else halves(left)
    right_high, right_low = right if isinstance(right, tuple) else halves(right)
    dot = functools.partial(lax.dot_general, dimension_numbers=dims, preferred_element_type=F32)
    rows = left_high.shape[0]
    both = dot(jnp.concatenate([left_high, left_low], 0), right_high)
    return both[:rows] + both[rows:] + dot(left_high, right_low)


def ordered(mine, theirs, place, axis):
    first = jnp.where(place == 0, mine, theirs)
    second = jnp.where(place == 0, theirs, mine)
    return jnp.concatenate([first, second], axis)


VMEM_LIMIT = 20 * 1024 * 1024


def options(cost):
    return dict(
        cost_estimate=pl.CostEstimate(flops=cost * 1000000, bytes_accessed=0, transcendentals=0),
        compiler_params=pltpu.CompilerParams(vmem_limit_bytes=VMEM_LIMIT),
    )


def call(kernel, name, outs, args, scalars=1, scratch=(), cost=1000):
    in_specs = [pl.BlockSpec(memory_space=pltpu.SMEM)] * scalars
    in_specs += [pl.BlockSpec(memory_space=pltpu.VMEM)] * (len(args) - scalars)
    return pl.pallas_call(
        kernel,
        out_shape=[
            jax.ShapeDtypeStruct(*out) if isinstance(out[0], tuple) else jax.ShapeDtypeStruct(out, F32)
            for out in outs
        ],
        in_specs=in_specs,
        out_specs=[pl.BlockSpec(memory_space=pltpu.VMEM)] * len(outs),
        scratch_shapes=list(scratch),
        name=name,
        **options(cost),
    )(*args)


def put_halves(value, high_out, low_out, at):
    high, low = halves(value)
    high_out[at] = high
    low_out[at] = low


def split_kernel(own, partner, *outs):
    put_halves(own[0, 0].reshape(-1, own.shape[-1]), *outs[:2], 0)
    put_halves(partner[0, 0].reshape(-1, own.shape[-1]), *outs[2:], 0)


def split_tiles(level, own, partner):
    own = pltpu.with_memory_space_constraint(own, pltpu.HBM)
    owned, slots, depth, width = own.shape[1:]
    block_in = pl.BlockSpec((1, 1, slots, depth, width), lambda s: (level, s, 0, 0, 0))
    block_out = pl.BlockSpec((1, slots * depth, width), lambda s: (s, 0, 0))
    return pl.pallas_call(
        split_kernel,
        grid=(owned,),
        out_shape=[jax.ShapeDtypeStruct((owned, slots * depth, width), BF16)] * 4,
        in_specs=[block_in] * 2,
        out_specs=[block_out] * 4,
        name="split_tiles",
        **options(2000),
    )(own, partner)


def whole_diag(level, diags, s):
    own, partner, own_other, partner_other = diags
    half = own.shape[1]
    if s < half:
        pair = own[level, s], own_other[level - 1, s]
    else:
        pair = partner[level, s % half], partner_other[level - 1, s % half]
    return jnp.concatenate(pair, 0)


def diag_by_tiles(d0, d1, d2, d3, *refs):
    tiles, outs = refs[:4], refs[4:]
    half = d0.shape[1]
    for s in range(2 * half):
        value = dot3(whole_diag(1, (d0, d1, d2, d3), s), part_of(tiles, s), NT)
        put_halves(value, *(outs[:2] if s < half else outs[2:]), s % half)


def gram_by_tiles(d0, d1, d2, d3, *refs):
    tiles, grams, outs = refs[:4], refs[4], refs[5:]
    half = d0.shape[1]
    for s in range(2 * half):
        diag = whole_diag(2, (d0, d1, d2, d3), s)
        gram = dot3(diag.T, diag, NN)
        grams[s] = gram
        value = dot3(gram, part_of(tiles, s), NT)
        put_halves(value, *(outs[:2] if s < half else outs[2:]), s % half)


def part_of(parts, s):
    count = len(parts) // 2
    half = parts[0].shape[0]
    chosen = parts[:count] if s < half else parts[count:]
    return tuple(part[s % half] for part in chosen)


def split_first(diag, high, low):
    for s in range(high.shape[0]):
        put_halves(diag[0, s], high, low, s)


def first_values(rhs_own, rhs_other, diag_high, diag_low, mine, partner):
    core, col = lax.axis_index("rows") % 2, lax.axis_index("cols")
    half = mine.shape[1]
    for s in range(rhs_own.shape[0]):
        rows = ordered(rhs_own[s], rhs_other[s], col, 0)
        values = dot3((diag_high[s], diag_low[s]), rows, NN).T
        low, high = values[:half], values[half:]
        mine[s] = jnp.where(core == 0, low, high)
        partner[s] = jnp.where(core == 0, high, low)


def split_diag(diag):
    shape = diag.shape[1:]
    return pl.pallas_call(
        split_first,
        grid=(1,),
        out_shape=[jax.ShapeDtypeStruct(shape, BF16)] * 2,
        in_specs=[pl.BlockSpec((1,) + shape, lambda i: (0, 0, 0, 0))],
        out_specs=[pl.BlockSpec(shape, lambda i: (0, 0, 0))] * 2,
        name="split_diag",
        **options(500),
    )(pltpu.with_memory_space_constraint(diag, pltpu.HBM))


def slot_places(sources, counts, places):
    row = lax.axis_index("rows")
    levels, owned, slots = sources.shape
    total = lax.axis_size("rows") * owned
    for l in range(levels):
        for s in range(owned):
            for k in range(slots):
                source = sources[l, s, k]
                live = k < counts[l, s]
                lower = jnp.where(source >= total, 1, 0)
                within = source - lower * total
                place = (row ^ (within // owned)) * owned + within % owned
                at = s * slots + k
                if l == 0:
                    places[0, at] = jnp.where(live, place, -1)
                else:
                    places[1, at] = jnp.where(live & (lower == 0), place, -1)
                    places[2, at] = jnp.where(live & (lower == 1), place, -1)


def place_of(places, index, slot, owned):
    own, partner = places
    count = own.shape[1]
    if slot < count:
        place = own[index, slot]
        return jnp.maximum(place, 0), place >= 0
    place = partner[index, slot - count]
    return jnp.where(place >= 0, place ^ owned, 0), place >= 0


def turned_rhs(rhs, mine, partner):
    core = lax.axis_index("rows") % 2
    half = mine.shape[2]
    for l in range(mine.shape[0]):
        for s in range(mine.shape[1]):
            rows = rhs[l + 1, s].T
            low, high = rows[:half], rows[half:]
            mine[l, s] = jnp.where(core == 0, low, high)
            partner[l, s] = jnp.where(core == 0, high, low)


def gathered(index, places, pieces, window):
    sups = pieces[0].shape[0]
    slots = 2 * places[0].shape[1] // sups
    for number, piece in enumerate(pieces):
        window[number * sups : (number + 1) * sups] = piece[...]
    for s in range(sups):
        picked = []
        for k in range(slots):
            place, live = place_of(places, index, s * slots + k, sups // 2)
            picked.append(jnp.where(live, window[place], 0.0))
        yield jnp.concatenate(picked, 1)


def upper_of(level, mine, partner, s):
    half = mine.shape[1]
    return mine[level - 1, s] if s < half else partner[level - 1, s % half]


def update_lower(index, level, places, places_partner, rhs, rhs_partner, *refs):
    tiles, pieces, (out, window) = refs[:4], refs[4:-2], refs[-2:]
    col = lax.axis_index("cols")
    for s, left in enumerate(gathered(index, (places, places_partner), pieces, window)):
        right = upper_of(level, rhs, rhs_partner, s)
        zero = jnp.zeros_like(right)
        base = jnp.concatenate([jnp.where(col == 0, right, zero), jnp.where(col == 0, zero, right)], 1)
        out[s] = base - dot3(left, part_of(tiles, s), NN)


def middle_values(residual, d0, d1, d2, d3, own, other):
    depth = own.shape[2]
    for s in range(own.shape[0]):
        values = dot3(residual[s], whole_diag(1, (d0, d1, d2, d3), s), NT)
        own[s] = values[:, :depth]
        other[s] = values[:, depth:]


def update_top(places, places_partner, *refs):
    tiles, base, pieces, (out, window) = refs[:4], refs[4], refs[5:-2], refs[-2:]
    for s, left in enumerate(gathered(2, (places, places_partner), pieces, window)):
        out[s] = base[s] - dot3(left, part_of(tiles, s), NN)


def add_terms(index, places, tiles, left, s, totals):
    owned = tiles[0].shape[0]
    depth = totals.shape[2]
    terms = dot3(left, part_of(tiles, s), NN)
    slots = terms.shape[1] // depth
    for k in range(slots):
        place, live = place_of(places, index, s * slots + k, owned)
        term = jnp.where(live, terms[:, k * depth : (k + 1) * depth], 0.0)
        totals[place] = totals[place] + term


def share_out(col, x, s, solved_mine, solved_partner):
    depth = solved_mine.shape[2]
    half = solved_mine.shape[0]
    share = jnp.where(col == 0, x[:, :depth], x[:, depth:])
    if s < half:
        solved_mine[s] = share
    else:
        solved_partner[s % half] = share


def pieces_out(totals, outs):
    first = 0
    for out in outs:
        out[...] = totals[first : first + out.shape[0]]
        first += out.shape[0]


def top_carry(places, places_partner, mine, theirs, t0, t1, t2, t3, residual, *rest):
    outs, totals = rest[:-1], rest[-1]
    totals[...] = jnp.zeros_like(totals)
    for s in range(residual.shape[0]):
        left = mine[s] + theirs[s]
        residual[s] = left
        add_terms(2, (places, places_partner), (t0, t1, t2, t3), left, s, totals)
    pieces_out(totals, outs)


def lowest_carry(
    places, places_partner, residual, t0, t1, t2, t3, grams,
    totals, solved_mine, solved_partner,
):
    totals[...] = jnp.zeros_like(totals)
    col = lax.axis_index("cols")
    for s in range(residual.shape[0]):
        share_out(col, dot3(residual[s], grams[s], NN), s, solved_mine, solved_partner)
        add_terms(1, (places, places_partner), (t0, t1, t2, t3), residual[s], s, totals)


def middle_carry(
    places, places_partner, own, other, d0, d1, d2, d3, t0, t1, t2, t3,
    lowest, solved_mine, solved_partner, *rest
):
    outs, totals = rest[:-1], rest[-1]
    totals[...] = lowest[...]
    for s in range(own.shape[0]):
        left = jnp.concatenate([own[s], other[s]], 1)
        add_terms(0, (places, places_partner), (t0, t1, t2, t3), left, s, totals)
        x = dot3(left, whole_diag(1, (d0, d1, d2, d3), s), NN)
        share_out(lax.axis_index("cols"), x, s, solved_mine, solved_partner)
    pieces_out(totals, outs)


def last_product(values, a, b, c, d, e, d_own, d_partner, mine, partner):
    sups = values.shape[0]
    half = sups // 2
    for s in range(sups):
        carried = a[s] + b[s] + c[s] + d[s] + e[s]
        diag, out = (d_own, mine) if s < half else (d_partner, partner)
        out[s % half] = dot3(values[s] - carried, diag[0, s % half], NN)


def turned_solution(mine, partner, own, other):
    core, col = lax.axis_index("rows") % 2, lax.axis_index("cols")
    depth = own.shape[1]
    for s in range(mine.shape[0]):
        both = ordered(mine[s], partner[s], core, 0)
        low, high = both[:, :depth].T, both[:, depth:].T
        own[s] = jnp.where(col == 0, low, high)
        other[s] = jnp.where(col == 0, high, low)


def turned_upper(mine2, partner2, mine1, partner1, out):
    core = lax.axis_index("rows") % 2
    for s in range(mine2.shape[0]):
        out[0, s] = ordered(mine1[s], partner1[s], core, 0).T
        out[1, s] = ordered(mine2[s], partner2[s], core, 0).T


def local(rhs, diag_inv, factor_tiles, tile_source, tile_count):
    levels, owned, share_rows, columns = rhs.shape
    slots = tile_source.shape[2]
    sups = 2 * owned
    block = share_rows * 2
    half_columns = columns // 2
    rows_total = lax.axis_size("rows")
    piece = (sups, half_columns, share_rows)
    shared = (owned, half_columns, share_rows)
    window = (PIECES * sups, half_columns, share_rows)
    after = lax.optimization_barrier

    def swap_cols(value):
        return lax.ppermute(value, "cols", [(0, 1), (1, 0)])

    def swap_rows(value, bits):
        return lax.ppermute(value, "rows", [(r, r ^ bits) for r in range(rows_total)])

    def swap_core(value):
        return swap_rows(value, 1)

    def swap_x(value):
        return swap_rows(value, 2)

    def swap_mid(value):
        low, high = rows_total // 4, 3 * rows_total // 4
        pairs = [(r, r ^ 12 if low <= r < high else r ^ 2) for r in range(rows_total)]
        return lax.ppermute(value, "rows", pairs)

    def gather_pieces(value):
        far = swap_rows(value, 8)
        beside = swap_x(value)
        mid = swap_mid(value)
        near = swap_rows(value, 4)
        return [
            value, beside, near, swap_rows(beside, 4), far, swap_x(far), mid, swap_mid(beside)
        ]

    def scatter_upper(p):
        far = swap_rows(p[4] + swap_x(p[5]), 8)
        beside = swap_x(p[1] + (swap_mid(p[7]) + swap_rows(p[3], 4)))
        mid = swap_mid(p[6])
        near = swap_rows(p[2], 4)
        return [p[0], far, beside, mid, near]

    def scatter_lowest(p):
        far = swap_rows(p[4] + swap_x(p[5]), 8)
        beside = swap_x(p[1] + (swap_mid(p[7]) + swap_rows(p[3], 4)))
        mid = swap_mid(p[6])
        near = swap_rows(p[2], 4)
        return [p[0], mid, near, beside, far]

    rhs0 = rhs[0]
    rhs0_other = swap_cols(rhs0)
    d_partner = swap_core(diag_inv)
    tiles_partner = swap_core(factor_tiles)
    d_low = split_diag(diag_inv)
    upper_diag = diag_inv[1:]
    d_other = swap_cols(upper_diag)
    tile_source, upper_diag, rhs0 = after((tile_source, upper_diag, rhs0))
    own_places = pl.pallas_call(
        slot_places,
        out_shape=jax.ShapeDtypeStruct((levels, owned * slots), jnp.int32),
        in_specs=[pl.BlockSpec(memory_space=pltpu.SMEM)] * 2,
        out_specs=pl.BlockSpec(memory_space=pltpu.SMEM),
        name="slot_places",
        **options(500),
    )(tile_source, tile_count)
    places = [own_places, swap_core(own_places)]
    rhs0, places, tiles_partner, d_partner, d_low = after(
        (rhs0, places, tiles_partner, d_partner, d_low)
    )
    mine, partner = call(first_values, "first_values", [shared] * 2, [rhs0, rhs0_other, *d_low], 0)
    values0 = jnp.concatenate([mine, swap_core(partner)], 0)
    upper, upper_partner = call(
        turned_rhs, "turned_rhs", [(levels - 1, owned, half_columns, share_rows)] * 2, [rhs], 0
    )
    uppers = [upper, swap_core(upper_partner)]
    values0, uppers = after((values0, uppers))
    pieces0 = gather_pieces(values0)

    reach = slots * share_rows
    wide = [((owned, block, reach), BF16)] * 4
    low_tiles = split_tiles(0, factor_tiles, tiles_partner)
    full = (sups, half_columns, block)
    scratch = [pltpu.VMEM(window, F32)]
    d_other, _ = after((d_other, (low_tiles, uppers, pieces0)))
    diags = [diag_inv, d_partner, d_other, swap_core(d_other)]
    partial = call(
        functools.partial(update_lower, 0, 1), "update_middle", [full],
        [*places, *uppers, *low_tiles, *pieces0], 2, scratch,
    )[0]
    own, other = call(middle_values, "middle_values", [piece] * 2, [partial, *diags], 0)
    low_ready, _ = after((low_tiles, other))
    low_turned = call(diag_by_tiles, "diag_by_tiles", wide, [*diags, *low_ready], 0, cost=3000)
    own, low_turned = after((own, low_turned))
    values1 = own + swap_cols(other)
    pieces1 = gather_pieces(values1)
    tiles, _ = after((factor_tiles, values1))
    top_tiles = split_tiles(1, tiles, tiles_partner)
    base = call(
        functools.partial(update_lower, 1, 2), "update_top_low", [full],
        [*places, *uppers, *top_tiles, *pieces0], 2, scratch,
    )[0]

    partial = call(
        update_top, "update_top", [full], [*places, *top_tiles, base, *pieces1], 2, scratch
    )[0]
    top_ready, _ = after((top_tiles, partial))
    grams, *top_turned = call(
        gram_by_tiles, "gram_by_tiles", [(sups, block, block)] + wide, [*diags, *top_ready], 0,
        cost=3000,
    )
    residual, *out = call(
        top_carry, "top_carry", [full] + [piece] * PIECES,
        [*places, partial, swap_cols(partial), *top_turned], 2, scratch,
    )
    carried = values1 - functools.reduce(jnp.add, scatter_upper(out))
    residual, _ = after((residual, carried))
    lowest, mine2, partner2 = call(
        lowest_carry, "lowest_carry", [window, shared, shared],
        [*places, residual, *top_turned, grams], 2, cost=2000,
    )

    mine1, partner1, *out = call(
        middle_carry, "middle_carry", [shared, shared] + [piece] * PIECES,
        [*places, carried, swap_cols(carried), *diags, *low_turned, lowest],
        2, scratch,
    )

    mine, partner = call(
        last_product, "last_product", [(owned, half_columns, block)] * 2,
        [values0, *scatter_lowest(out), diag_inv, d_partner], 0,
    )
    own, other = call(
        turned_solution, "turned_solution", [(owned, share_rows, columns)] * 2,
        [mine, swap_core(partner)], 0,
    )
    own = own + swap_cols(other)

    partner1, partner2, _ = after((partner1, partner2, mine))
    result_upper = call(
        turned_upper, "turned_upper", [(levels - 1, owned, share_rows, columns)],
        [mine2, swap_core(partner2), mine1, swap_core(partner1)], 0,
    )[0]
    return jnp.concatenate([own[None], result_upper], 0)


def solution(mesh):
    placed = (
        P(None, "rows", "cols", None),
        P(None, "rows", "cols", None),
        P(None, "rows", None, "cols", None),
        P(None, "rows", None),
        P(None, "rows"),
    )
    small = mesh.shape["rows"] == 16 and mesh.shape["cols"] == 2
    return jax.shard_map(
        local if small else local_any,
        mesh=mesh,
        in_specs=placed,
        out_specs=P(None, "rows", "cols", None),
        check_vma=False,
    )
```
